32 devices in a mesh: ctx: 8 (over z, core), fsdp: 4 (over y, x).
Axes of the slice: x: 2, y: 2, z: 4, core: 2. Of those that a mesh axis runs over, the one named last changes fastest.
Arguments:
- hidden_in: bfloat16 [8, 2048, 2048], P('fsdp', 'ctx'), may hold values from -6 to 6
- cotangent: bfloat16 [8, 2048, 2048], P('fsdp', 'ctx'), may hold values from -6 to 6
- segment_ids: int32 [8, 2048], P('fsdp'), may hold values from 0 to 8, as said below
- w_query: bfloat16 [2048, 2048], P('fsdp'), may hold values from -0.25 to 0.25
- w_key: bfloat16 [2048, 1024], P('fsdp'), may hold values from -0.125 to 0.125
- w_value: bfloat16 [2048, 1024], P('fsdp'), may hold values from -0.125 to 0.125
- w_output: bfloat16 [2048, 2048], P('fsdp'), may hold values from -0.75 to 0.75
- w_gate: bfloat16 [2048, 8192], P('fsdp'), may hold values from -0.125 to 0.125
- w_up: bfloat16 [2048, 8192], P('fsdp'), may hold values from -0.125 to 0.125
- w_down: bfloat16 [8192, 2048], P('fsdp'), may hold values from -0.125 to 0.125
- attn_gain: bfloat16 [2048], P('fsdp'), may hold values from 0.5 to 1.5
- ffn_gain: bfloat16 [2048], P('fsdp'), may hold values from 0.5 to 1.5
Outputs:
- layer_out: bfloat16 [8, 2048, 2048], P('fsdp', 'ctx')
- grad_in: bfloat16 [8, 2048, 2048], P('fsdp', 'ctx')
- grad_query: float32 [2048, 2048], P('fsdp')
- grad_key: float32 [2048, 1024], P('fsdp')
- grad_value: float32 [2048, 1024], P('fsdp')
- grad_output: float32 [2048, 2048], P('fsdp')
- grad_gate: float32 [2048, 8192], P('fsdp')
- grad_up: float32 [2048, 8192], P('fsdp')
- grad_down: float32 [8192, 2048], P('fsdp')
- grad_attn_gain: float32 [2048], P('fsdp')
- grad_ffn_gain: float32 [2048], P('fsdp')
The draws below stay inside these ranges and needn't reach their ends.
Inputs may be any that keep to these rules, and one draw needn't show every extreme that they name: `segment_ids`: in each group the first 1024 positions are 0; continuations 1 to 8 follow in order, each of 64 to 192 positions; in each group one has exactly 192 positions and one exactly 64.
All inputs are finite; a program needn't handle non-finite values.
Results may differ from the reference program's by a relative error of at most 0.02.
Values may be sent and summed in bfloat16 or wider, within the bound.
No kernel may reach another device: no remote copies, remote signals or barrier semaphores. Data moves between devices by JAX's collectives and lax.ppermute only.
A program may use at most 832 MiB of HBM per device.

```python
import math
import jax
import jax.numpy as jnp
from jax import lax

D = 2048
HEADS = 16
KVH = 8
HD = 128
FF = 8192
PROMPT = 1024
CONT = 8
CLEN = 128
QD = 2048
KVD = 1024
GT = 2048
GROUPS = 8


def draw_segment_ids(key, part):

    def one_group(index):
        seeded = jax.random.fold_in(key, index)
        pairs = CONT // 2
        shifts = jax.random.randint(jax.random.fold_in(seeded, 1), (pairs,), -(CLEN // 2), CLEN // 2 + 1)
        chosen = jax.random.randint(jax.random.fold_in(seeded, 2), (), 0, pairs)
        flipped = jax.random.randint(jax.random.fold_in(seeded, 3), (), 0, 2)
        forced = CLEN // 2 * (1 - 2 * flipped)
        shifts = jnp.where(jnp.arange(pairs) == chosen, forced, shifts)
        lengths = jnp.stack([CLEN + shifts, CLEN - shifts], axis=1).reshape(CONT)
        ends = PROMPT + jnp.cumsum(lengths)
        position = jnp.arange(GT)
        inside = (position >= PROMPT).astype(jnp.int32)
        passed = jnp.sum((position[:, None] >= ends[None, :CONT - 1]).astype(jnp.int32), axis=1)
        return (inside + passed).astype(jnp.int32)
    return jax.vmap(one_group)(jnp.arange(GROUPS))


def levels(rng, shape, split, low, largest):
    def one(dim, shards_of):
        draws = jax.random.uniform(jax.random.fold_in(jax.random.fold_in(rng, 6), dim), (shards_of,), jnp.float32, low / len(split), largest / len(split))
        return jnp.repeat(jnp.exp(draws), shape[dim] // shards_of).reshape((-1,) + (1,) * (len(shape) - dim - 1))

    loudness = one(*split[0])
    for cut in split[1:]:
        loudness = loudness * one(*cut)
    return loudness


def noise(rng, extent, spread, bound, split=(), kind=jnp.bfloat16):
    level = levels(rng, extent, split, -0.22, 0.18) if split else 1.0
    entries = jax.random.normal(rng, extent, jnp.float32) * spread * level
    return jnp.minimum(jnp.maximum(entries, -bound), bound).astype(kind)


def setup_inputs(seed: int = 0) -> dict:
    splits = jax.random.split(jax.random.key(seed), 13)
    return {
        "hidden_in": noise(splits[0], (GROUPS, GT, D), 1.0, 6.0, ((0, 4), (1, 8))),
        "cotangent": noise(splits[1], (GROUPS, GT, D), 1.0, 6.0, ((0, 4), (1, 8))),
        "segment_ids": draw_segment_ids(jax.random.fold_in(splits[12], 71), 0),
        "w_query": noise(splits[3], (D, QD), (D // 4) ** -0.5, 0.25, ((0, 4),)),
        "w_key": noise(splits[4], (D, KVD), D ** -0.5, 0.125, ((0, 4),)),
        "w_value": noise(splits[5], (D, KVD), D ** -0.5, 0.125, ((0, 4),)),
        "w_output": noise(splits[6], (QD, D), (QD // 32) ** -0.5, 0.75, ((0, 4),)),
        "w_gate": noise(splits[7], (D, FF), D ** -0.5, 0.125, ((0, 4),)),
        "w_up": noise(splits[8], (D, FF), D ** -0.5, 0.125, ((0, 4),)),
        "w_down": noise(splits[9], (FF, D), (FF // 4) ** -0.5, 0.125, ((0, 4),)),
        "attn_gain": jnp.clip(1.0 + 0.1 * jax.random.normal(splits[10], (D,), jnp.float32), 0.5, 1.5).astype(jnp.bfloat16),
        "ffn_gain": jnp.clip(1.0 + 0.1 * jax.random.normal(splits[11], (D,), jnp.float32), 0.5, 1.5).astype(jnp.bfloat16),
    }


@jax.custom_vjp
def low(v):
    return lax.optimization_barrier(v.astype(jnp.bfloat16)).astype(jnp.float32)

@jax.custom_vjp
def low_back(v):
    return v

def low_keep(v):
    return (low(v), None)

def low_pass(kept, grad):
    return (grad,)

def back_keep(v):
    return (v, None)

def back_low(kept, grad):
    return (low(grad),)
low.defvjp(low_keep, low_pass)
low_back.defvjp(back_keep, back_low)
eps_norm = 1e-05
rope_base = 1000000.0
mask_fill = -1e+30
highest = lax.Precision.HIGHEST

def matmul(left, right):
    return jnp.dot(left, right, precision=highest)

def norm_rows(values, gain):
    inverse = lax.rsqrt(lax.optimization_barrier(jnp.mean(values * values, axis=-1, keepdims=True)) + eps_norm)
    return values * inverse * gain

def positions_of(segments):
    labels = jnp.arange(CONT + 1, dtype=jnp.int32)
    table = (segments[:, None] == labels[None, :]).astype(jnp.int32)
    counts = lax.optimization_barrier(jnp.sum(table, axis=0))
    starts = jnp.cumsum(counts) - counts
    leading = lax.optimization_barrier(jnp.sum(table * starts[None, :], axis=1))
    index = jnp.arange(segments.shape[0], dtype=jnp.int32)
    return index - leading + jnp.where(segments > 0, PROMPT, 0).astype(jnp.int32)

def rotary_tables(positions):
    half_width = HD // 2
    frequency = rope_base ** (-(jnp.arange(half_width, dtype=jnp.float32) * 2.0) / HD)
    angles = positions.astype(jnp.float32)[:, None] * frequency[None, :]
    return (jnp.cos(angles), jnp.sin(angles))

def rotate(values, cosine, sine, direction):
    rows_count = values.shape[0]
    heads_view = values.reshape(rows_count, -1, HD)
    former = heads_view[..., :HD // 2]
    latter = heads_view[..., HD // 2:]
    cos_part = cosine[:, None, :]
    sin_part = sine[:, None, :] * direction
    turned = jnp.concatenate([former * cos_part - latter * sin_part, latter * cos_part + former * sin_part], axis=-1)
    return turned.reshape(rows_count, -1)

def attend(queries, keys_all, values_all, segments):
    tokens = queries.shape[0]
    query_view = queries.reshape(tokens, KVH, HEADS // KVH, HD)
    key_view = keys_all.reshape(tokens, KVH, HD)
    value_view = values_all.reshape(tokens, KVH, HD)
    scores = jnp.einsum('qhgd,khd->hgqk', query_view, key_view, precision=highest) * (1.0 / math.sqrt(HD))
    scores = low_back(scores)
    index = jnp.arange(tokens, dtype=jnp.int32)
    visible = (index[None, :] <= index[:, None]) & ((segments[None, :] == segments[:, None]) | (segments[None, :] == 0))
    probs = jax.nn.softmax(jnp.where(visible[None, None], scores, mask_fill), axis=-1)
    mixed = jnp.einsum('hgqk,khd->qhgd', low(probs), value_view, precision=highest)
    return mixed.reshape(tokens, QD)

def group_forward(hidden, segments, params):
    w_query, w_key, w_value, w_output, w_gate, w_up, w_down, attn_gain, ffn_gain = params
    cosine, sine = rotary_tables(positions_of(segments))
    normed = low(norm_rows(hidden, attn_gain))
    queries = low(rotate(low_back(matmul(normed, w_query)), cosine, sine, 1.0))
    keys_all = low(rotate(low_back(matmul(normed, w_key)), cosine, sine, 1.0))
    values_all = low(low_back(matmul(normed, w_value)))
    mixed = low(low_back(attend(queries, keys_all, values_all, segments)))
    middle = hidden + low_back(matmul(mixed, w_output))
    ffn_in = low(norm_rows(middle, ffn_gain))
    gate_pre = low_back(matmul(ffn_in, w_gate))
    up_pre = low_back(matmul(ffn_in, w_up))
    hidden_act = low(jax.nn.silu(gate_pre) * up_pre)
    return middle + low_back(matmul(hidden_act, w_down))

def reference(hidden_in, cotangent, segment_ids, w_query, w_key, w_value, w_output, w_gate, w_up, w_down, attn_gain, ffn_gain):
    params = tuple((weight.astype(jnp.float32) for weight in (w_query, w_key, w_value, w_output, w_gate, w_up, w_down, attn_gain, ffn_gain)))
    checked = jax.checkpoint(group_forward)

    def forward(hidden, weights):

        def scan_step(state_carry, inputs):
            return (state_carry, checked(inputs[0], inputs[1], weights))
        unused, result = lax.scan(scan_step, jnp.zeros((), jnp.float32), (hidden, segment_ids))
        return result
    result, pullback = jax.vjp(forward, hidden_in.astype(jnp.float32), params)
    grad_hidden, grads = pullback(cotangent.astype(jnp.float32))
    return (result.astype(jnp.bfloat16), grad_hidden.astype(jnp.bfloat16), grads[0], grads[1], grads[2], grads[3], grads[4], grads[5], grads[6], grads[7], grads[8])
```

```python
import functools
import math

import jax
import jax.numpy as jnp
from jax import lax
from jax.experimental import pallas as pl
from jax.experimental.pallas import tpu as pltpu
from jax.sharding import PartitionSpec as P

HD = 128
PROMPT = 1024
CONT = 8
LONGEST = 192

eps_norm = 1e-05
rope_base = 1000000.0
mask_fill = -1e30
log2_e = 1.4426950408889634
bf16 = jnp.bfloat16
f32 = jnp.float32
i32 = jnp.int32
MIB = 1024 * 1024
SMALL = pl.CostEstimate(flops=0, bytes_accessed=0, transcendentals=0)


def positions_of(segments, first_row, block):
    own = lax.dynamic_slice_in_dim(segments, first_row, block)
    leading = jnp.sum((segments[None, :] < own[:, None]).astype(i32), axis=1)
    index = first_row + jnp.arange(block, dtype=i32)
    return jnp.where(own > 0, index - leading + PROMPT, index)


def rotary_tables(positions):
    half_width = HD // 2
    frequency = rope_base ** (-(jnp.arange(half_width, dtype=f32) * 2.0) / HD)
    angles = positions.astype(f32)[:, None] * frequency[None, :]
    cosine, sine = jnp.cos(angles), jnp.sin(angles)
    return (
        jnp.concatenate([cosine, cosine], axis=1),
        jnp.concatenate([-sine, sine], axis=1),
    )


def norm_parts(values, gain):
    inverse = lax.rsqrt(jnp.mean(values * values, axis=-1, keepdims=True) + eps_norm)
    scaled = values * inverse
    return (scaled * gain, scaled, inverse)


def norm_back(grad_out, values, scaled, inverse, gain):
    grad_scaled = grad_out * gain
    grad_gain = jnp.sum(grad_out * scaled, axis=0)
    along = jnp.mean(grad_scaled * values, axis=-1, keepdims=True)
    grad_values = inverse * grad_scaled - values * inverse * inverse * inverse * along
    return (grad_values, grad_gain)


def dot(left, right, dims, out=f32):
    return lax.dot_general(left, right, (dims, ((), ())), preferred_element_type=out)


def nn(left, right, out=f32):
    return dot(left, right, ((1,), (0,)), out)


def nt(left, right, out=f32):
    return dot(left, right, ((1,), (1,)), out)


def tn(left, right, out=f32):
    return dot(left, right, ((0,), (0,)), out)


def product_kernel(left_ref, right_ref, o_ref):
    o_ref[...] = tn(left_ref[0], right_ref[0]).astype(bf16)


def product(left, right):
    left = left[None] if left.ndim == 2 else left
    right = right[None] if right.ndim == 2 else right
    lefts, depth, count = left.shape
    stack, _, cols = right.shape
    side = min(count, cols, 1024)
    across = cols // side
    return pl.pallas_call(
        product_kernel,
        out_shape=jax.ShapeDtypeStruct((count, stack * cols), bf16),
        grid=(stack, count // side, across),
        in_specs=[
            pl.BlockSpec((1, depth, side), lambda n, i, j: (n % lefts, 0, i)),
            pl.BlockSpec((1, depth, side), lambda n, i, j: (n, 0, j)),
        ],
        out_specs=pl.BlockSpec((side, side), lambda n, i, j: (i, n * across + j)),
        compiler_params=pltpu.CompilerParams(vmem_limit_bytes=48 * MIB),
        cost_estimate=SMALL,
    )(left, right)


def turned(u, cosine, sine):
    return u * cosine + pltpu.roll(u, HD // 2, 1) * sine


def project_kernel(x_ref, first_ref, last_ref, cos_ref, sin_ref, o_ref, *, second):
    acc = nn(x_ref[...], jnp.concatenate([first_ref[...], last_ref[...]], axis=1))
    cosine, sine = cos_ref[...], sin_ref[...]
    o_ref[:, :HD] = turned(acc[:, :HD], cosine, sine).astype(bf16)
    last = acc[:, HD:]
    if second:
        last = turned(last, cosine, sine)
    o_ref[:, HD:] = last.astype(bf16)


def project(x, weight, cosine, sine, second):
    count, depth = x.shape
    cols = weight.shape[1]
    steps = cols // (2 * HD)
    whole = lambda i: (0, 0)
    first = (lambda i: (0, 2 * i)) if second else (lambda i: (0, i))
    last = (lambda i: (0, 2 * i + 1)) if second else (lambda i: (0, i + steps))
    return pl.pallas_call(
        functools.partial(project_kernel, second=second),
        out_shape=jax.ShapeDtypeStruct((count, cols), bf16),
        grid=(steps,),
        in_specs=[
            pl.BlockSpec((count, depth), whole),
            pl.BlockSpec((depth, HD), first),
            pl.BlockSpec((depth, HD), last),
            pl.BlockSpec((count, HD), whole),
            pl.BlockSpec((count, HD), whole),
        ],
        out_specs=pl.BlockSpec((count, 2 * HD), lambda i: (0, i)),
        compiler_params=pltpu.CompilerParams(vmem_limit_bytes=32 * MIB),
        cost_estimate=SMALL,
    )(x, weight, weight, cosine, sine)


def unturn_kernel(x_ref, cos_ref, sin_ref, o_ref):
    keys = pl.program_id(0) < pl.num_programs(0) // 2

    @pl.when(keys)
    def _():
        o_ref[...] = turned(x_ref[...].astype(f32), cos_ref[...], -sin_ref[...]).astype(bf16)

    @pl.when(jnp.logical_not(keys))
    def _():
        o_ref[...] = x_ref[...]


def unturn(x, cosine, sine):
    count, cols = x.shape
    heads = cols // (2 * HD)
    whole = lambda i: (0, 0)
    return pl.pallas_call(
        unturn_kernel,
        out_shape=jax.ShapeDtypeStruct((count, cols), bf16),
        grid=(2 * heads,),
        in_specs=[
            pl.BlockSpec((count, HD), lambda i: (0, jnp.where(i < heads, 2 * i, 2 * (i - heads) + 1))),
            pl.BlockSpec((count, HD), whole),
            pl.BlockSpec((count, HD), whole),
        ],
        out_specs=pl.BlockSpec((count, HD), lambda i: (0, i)),
    )(x, cosine, sine)


def stacked(ref):
    return jnp.concatenate([ref[:, :HD], ref[:, HD:]], axis=0)


def scores_of(keys, bias, queries):
    s = nt(keys, queries) * (log2_e / math.sqrt(HD))
    return s + jnp.concatenate([bias, bias], axis=1)


def key_rows(places, n, block):
    return pl.ds(pl.multiple_of(places[n] * block, block), block)


def attend_kernel(flags, places, bias_ref, q_ref, kv_ref, o_ref, lse_ref, m_ref, l_ref, acc_ref):
    queries = stacked(q_ref)
    block = q_ref.shape[0]
    m_ref[...] = jnp.full_like(m_ref, mask_fill)
    l_ref[...] = jnp.zeros_like(l_ref)
    acc_ref[...] = jnp.zeros_like(acc_ref)
    for n in range(bias_ref.shape[0] // block):

        @pl.when(flags[n] > 0)
        def _():
            at = key_rows(places, n, block)
            s = scores_of(kv_ref[at, :HD], bias_ref[n * block : (n + 1) * block, :], queries)
            m_old = m_ref[...]
            m_new = jnp.maximum(m_old, jnp.max(s, axis=0, keepdims=True))
            p = jnp.exp2(s - m_new)
            alpha = jnp.exp2(m_old - m_new)
            l_ref[...] = l_ref[...] * alpha + jnp.sum(p, axis=0, keepdims=True)
            acc_ref[...] = acc_ref[...] * alpha + tn(kv_ref[at, HD:], p.astype(bf16))
            m_ref[...] = m_new

    total = l_ref[...]
    out = (acc_ref[...] / total).T.astype(bf16)
    o_ref[:, :HD] = out[:block]
    o_ref[:, HD:] = out[block:]
    lse_ref[0] = m_ref[...] + jnp.log(total) * log2_e


def attend(flags, places, bias, queries, kv, m, block):
    tokens, cols = kv.shape
    heads = cols // (2 * HD)
    keys = bias.shape[0]
    return pl.pallas_call(
        attend_kernel,
        out_shape=(
            jax.ShapeDtypeStruct((block, cols), bf16),
            jax.ShapeDtypeStruct((heads, 1, 2 * block), f32),
        ),
        grid=(heads,),
        in_specs=[
            pl.BlockSpec(memory_space=pltpu.SMEM),
            pl.BlockSpec(memory_space=pltpu.SMEM),
            pl.BlockSpec((keys, block), lambda h: (0, 0)),
            pl.BlockSpec((block, 2 * HD), lambda h: (m, h)),
            pl.BlockSpec((tokens, 2 * HD), lambda h: (0, h)),
        ],
        out_specs=(
            pl.BlockSpec((block, 2 * HD), lambda h: (0, h)),
            pl.BlockSpec((1, 1, 2 * block), lambda h: (h, 0, 0)),
        ),
        scratch_shapes=[
            pltpu.VMEM((1, 2 * block), f32),
            pltpu.VMEM((1, 2 * block), f32),
            pltpu.VMEM((HD, 2 * block), f32),
        ],
        compiler_params=pltpu.CompilerParams(vmem_limit_bytes=32 * MIB),
        cost_estimate=SMALL,
    )(flags, places, bias, queries, kv)


def attend_back_kernel(
    flags,
    places,
    bias_ref,
    q_ref,
    kv_ref,
    o_ref,
    go_ref,
    lse_ref,
    cos_ref,
    sin_ref,
    gq_ref,
    gshared_ref,
    gnear_ref,
    acc_ref,
):
    queries = stacked(q_ref)
    block = q_ref.shape[0]
    grads = stacked(go_ref)
    product = grads.astype(f32) * stacked(o_ref).astype(f32)
    delta = jnp.sum(product.T, axis=0, keepdims=True)
    lse = lse_ref[0]
    acc_ref[...] = jnp.zeros_like(acc_ref)
    scale = 1.0 / math.sqrt(HD)
    for n in range(bias_ref.shape[0] // block):
        shared = gshared_ref.shape[0] // block
        to_ref, k = (gshared_ref, n) if n < shared else (gnear_ref, n - shared)
        to = slice(k * block, (k + 1) * block)

        @pl.when(flags[n] > 0)
        def _():
            at = key_rows(places, n, block)
            p = jnp.exp2(scores_of(kv_ref[at, :HD], bias_ref[n * block : (n + 1) * block, :], queries) - lse)
            gp = nt(kv_ref[at, HD:], grads)
            gs = (p * (gp - delta)).astype(bf16)
            acc_ref[...] += tn(kv_ref[at, :HD], gs)
            to_ref[to, :HD] = (nn(gs, queries) * scale).astype(bf16)
            to_ref[to, HD:] = nn(p.astype(bf16), grads).astype(bf16)

        @pl.when(flags[n] == 0)
        def _():
            to_ref[to, :] = jnp.zeros((block, 2 * HD), bf16)

    out = acc_ref[...].T * scale
    cosine, sine = cos_ref[...], -sin_ref[...]
    gq_ref[:, :HD] = turned(out[:block], cosine, sine).astype(bf16)
    gq_ref[:, HD:] = turned(out[block:], cosine, sine).astype(bf16)


def attend_back(flags, places, bias, queries, kv, mixed, grad_mixed, lse, cosine, sine, m, block):
    tokens, cols = kv.shape
    heads = cols // (2 * HD)
    keys = bias.shape[0]
    near = (near_count(block) + 1) * block
    own = pl.BlockSpec((block, 2 * HD), lambda h: (0, h))
    far = pl.BlockSpec((keys - near, 2 * HD), lambda h: (0, h))
    close = pl.BlockSpec((near, 2 * HD), lambda h: (0, h))
    return pl.pallas_call(
        attend_back_kernel,
        out_shape=(
            jax.ShapeDtypeStruct((block, cols), bf16),
            jax.ShapeDtypeStruct((keys - near, cols), bf16),
            jax.ShapeDtypeStruct((near, cols), bf16),
        ),
        grid=(heads,),
        in_specs=[
            pl.BlockSpec(memory_space=pltpu.SMEM),
            pl.BlockSpec(memory_space=pltpu.SMEM),
            pl.BlockSpec((keys, block), lambda h: (0, 0)),
            pl.BlockSpec((block, 2 * HD), lambda h: (m, h)),
            pl.BlockSpec((tokens, 2 * HD), lambda h: (0, h)),
            own,
            own,
            pl.BlockSpec((1, 1, 2 * block), lambda h: (h, 0, 0)),
            pl.BlockSpec((block, HD), lambda h: (m, 0)),
            pl.BlockSpec((block, HD), lambda h: (m, 0)),
        ],
        out_specs=(own, far, close),
        scratch_shapes=[pltpu.VMEM((HD, 2 * block), f32)],
        compiler_params=pltpu.CompilerParams(vmem_limit_bytes=40 * MIB),
        cost_estimate=SMALL,
    )(flags, places, bias, queries, kv, mixed, grad_mixed, lse, cosine, sine)


FCOLS = 256
FROWS = 512


def ffn_kernel(b_ref, gz_ref, wg_ref, wu_ref, wd_ref, act_ref, grads_ref, y_ref, gb_ref, yacc, gacc):
    step = pl.program_id(0)
    last = pl.num_programs(0) - 1

    @pl.when(step == 0)
    def _():
        yacc[...] = jnp.zeros_like(yacc)
        gacc[...] = jnp.zeros_like(gacc)

    def body(i, carry):
        at = pl.ds(pl.multiple_of(i * FROWS, FROWS), FROWS)
        w = jnp.concatenate([wg_ref[...], wu_ref[...]], axis=1)
        both = nn(b_ref[at, :], w)
        gate, up = both[:, :FCOLS], both[:, FCOLS:]
        grad_act = nt(gz_ref[0, at, :], wd_ref[...])
        sigma = jax.nn.sigmoid(gate)
        swish = gate * sigma
        act = (swish * up).astype(bf16)
        grad_gate = (grad_act * up * sigma * (1.0 + gate * (1.0 - sigma))).astype(bf16)
        grad_up = (grad_act * swish).astype(bf16)
        act_ref[at, :] = act
        grads_ref[0, at, :] = grad_gate
        grads_ref[1, at, :] = grad_up
        yacc[at, :] += nn(act, wd_ref[...])
        gacc[at, :] += nt(jnp.concatenate([grad_gate, grad_up], axis=1), w)
        return carry

    lax.fori_loop(0, b_ref.shape[0] // FROWS, body, 0)

    @pl.when(step == last)
    def _():
        y_ref[...] = yacc[...].astype(bf16)
        gb_ref[...] = gacc[...].astype(bf16)


def feed_forward(b, gz, gate_up, down, m, batches, kept):
    count, width = b.shape
    cols = down.shape[0]
    steps = cols // FCOLS
    once = pl.Buffered(1)
    wide = jax.ShapeDtypeStruct((batches * count, cols), bf16)
    narrow = jax.ShapeDtypeStruct((count, width), bf16)
    tile = pl.BlockSpec((count, FCOLS), lambda j: (m, j))
    total = pl.BlockSpec((count, width), lambda j: (0, 0), pipeline_mode=once)

    def kernel(*refs):
        ffn_kernel(*refs[:5], *refs[5 + len(kept) :])

    return pl.pallas_call(
        kernel,
        out_shape=(wide, jax.ShapeDtypeStruct((2,) + wide.shape, bf16), narrow, narrow),
        grid=(steps,),
        in_specs=[
            pl.BlockSpec((count, width), lambda j: (0, 0), pipeline_mode=once),
            pl.BlockSpec((1, count, width), lambda j: (0, 0, 0), pipeline_mode=once),
            pl.BlockSpec((width, FCOLS), lambda j: (0, j)),
            pl.BlockSpec((width, FCOLS), lambda j: (0, j + steps)),
            pl.BlockSpec((FCOLS, width), lambda j: (j, 0)),
        ]
        + [pl.BlockSpec(memory_space=pl.ANY)] * len(kept),
        out_specs=(tile, pl.BlockSpec((2, count, FCOLS), lambda j: (0, m, j)), total, total),
        scratch_shapes=[pltpu.VMEM((count, width), f32), pltpu.VMEM((count, width), f32)],
        input_output_aliases={5 + i: i for i in range(len(kept))},
        compiler_params=pltpu.CompilerParams(vmem_limit_bytes=60 * MIB),
        cost_estimate=SMALL,
    )(b, gz, gate_up, gate_up, down, *kept)


def plane():
    return lax.axis_size("fsdp")


def bits_of(n):
    return [1 << i for i in range(n.bit_length() - 1)]


def fswap(bits):
    return lambda value: lax.ppermute(value, "fsdp", [(i, i ^ bits) for i in range(plane())])


def cswap(bits):
    return lambda value: lax.ppermute(value, "ctx", [(i, i ^ bits) for i in range(lax.axis_size("ctx"))])


def move(pairs):
    pairs = list(pairs)
    return lambda value: lax.ppermute(value, "ctx", pairs)


def rows(value, start, size):
    return lax.dynamic_slice_in_dim(value, start, size, axis=0)


def put_rows(target, value, start):
    return lax.dynamic_update_slice_in_dim(target, value, start, axis=0)


def plus(left, right):
    return left.astype(f32) + right.astype(f32)


def joined(parts):
    return jnp.concatenate(parts, axis=0) if len(parts) > 1 else parts[0]


def blank(rows_count, cols, kind, source):
    anywhere = pl.BlockSpec(memory_space=pl.ANY)
    return pl.pallas_call(
        lambda source_ref, out_ref: None,
        out_shape=jax.ShapeDtypeStruct((rows_count, cols), kind),
        in_specs=[anywhere],
        out_specs=anywhere,
    )(source)


def gate(values):
    if len(values) < 2:
        return list(values)
    anywhere = pl.BlockSpec(memory_space=pl.ANY)
    out = pl.pallas_call(
        lambda *refs: None,
        out_shape=[jax.ShapeDtypeStruct(v.shape, v.dtype) for v in values],
        in_specs=[anywhere] * len(values),
        out_specs=[anywhere] * len(values),
        input_output_aliases={i: i for i in range(len(values))},
        cost_estimate=SMALL,
    )(*values)
    return list(out)


class Flow:
    def __init__(self, steps, fresh=False):
        self.steps, self.result, self.want, self.got = steps, None, [], None
        self.fresh = fresh
        self.go(None)

    def go(self, given):
        try:
            self.want = self.steps.send(given)
        except StopIteration as stop:
            self.want, self.result = [], stop.value


class Line:
    def __init__(self):
        self.under_way = []

    def launch(self, *flows):
        flows = [f for f in flows if f.want]
        ready = gate([value for f in flows if f.fresh for value, _ in f.want])
        for f in flows:
            f.got = [fn(ready.pop(0) if f.fresh else value) for value, fn in f.want]
            self.under_way.append(f)

    def settle(self, *held):
        gated = gate([a for f in self.under_way for a in f.got] + list(held))
        for f in self.under_way:
            given, gated = gated[: len(f.got)], gated[len(f.got) :]
            f.go(given)
        self.under_way = []
        return gated[0] if len(held) == 1 else gated

    def finish(self, *flows):
        if self.under_way:
            self.settle()
        while any(f.want for f in flows):
            self.launch(*flows)
            self.settle()


def order():
    out = []
    for bits in (bits_of(plane()), bits_of(plane())[::-1]):
        ds = [0]
        for b in bits:
            ds = ds + [d ^ b for d in ds]
        out += ds
    return out


def gather_flow(own):
    half = own.shape[0] // 2
    first, last = own[:half], own[half:]
    bits = bits_of(plane())
    for a, b in zip(bits, bits[::-1]):
        got = yield [(first, fswap(a)), (last, fswap(b))]
        first = joined([first, got[0]])
        last = joined([last, got[1]])
    return joined([first, last])


def scatter_flow(parts):
    total = parts.shape[0] // 2
    first, last = parts[:total], parts[total:]
    bits = bits_of(plane())
    for a, b in zip(bits[::-1], bits):
        n = first.shape[0] // 2
        got = yield [(first[n:].astype(bf16), fswap(a)), (last[n:].astype(bf16), fswap(b))]
        first = plus(first[:n], got[0])
        last = plus(last[:n], got[1])
    return joined([first, last])


def weight_flow(own):
    shard, cols = own.shape
    me = lax.axis_index("fsdp")
    core = lax.axis_index("ctx") % 2
    half, part = shard // 2, shard // 4
    full = None
    mine = rows(own, core * half, half)
    first, last = mine[:part], mine[part:]
    bits = bits_of(plane())
    held, pending = [0], []
    for a, b in zip(bits + [None], bits[::-1] + [None]):
        want = [(value, cswap(1)) for value, _, _ in pending]
        if a is not None:
            want += [(first, fswap(a)), (last, fswap(b))]
        got = yield want
        if full is None:
            full = put_rows(blank(shard * plane(), cols, bf16, got[0]), own, me * shard)
        for n, (here, ds, offset) in enumerate(pending):
            for k, d in enumerate(ds):
                at = slice(k * part, (k + 1) * part)
                start = (me ^ d) * shard + offset
                full = put_rows(full, here[at], start + core * half)
                full = put_rows(full, got[n][at], start + (1 - core) * half)
        if a is not None:
            order_a = held_of(bits[: bits.index(a)])
            order_b = held_of(bits[::-1][: bits[::-1].index(b)])
            n = len(pending)
            pending = [
                (got[n], [d ^ a for d in order_a], 0),
                (got[n + 1], [d ^ b for d in order_b], part),
            ]
            first = joined([first, got[n]])
            last = joined([last, got[n + 1]])
    return full


def held_of(bits):
    ds = [0]
    for b in bits:
        ds = ds + [d ^ b for d in ds]
    return ds


def column_flow(weights, full, left):
    me = lax.axis_index("fsdp")
    core = lax.axis_index("ctx") % 2
    planes = plane()
    shard = weights.shape[0]
    half = shard // 2
    size = weights.shape[1] // planes

    def columns(j, start, count):
        return lax.dynamic_slice(weights, (start, (me ^ j) * size), (count, size))

    got = yield [(columns(j, core * half, half), fswap(j)) for j in range(1, planes)]
    full[0] = lax.dynamic_update_slice(full[0], columns(0, 0, shard), (me * shard, left))
    other = yield [(piece, cswap(1)) for piece in got]
    for j in range(1, planes):
        start = (me ^ j) * shard
        full[0] = lax.dynamic_update_slice(full[0], got[j - 1], (start + core * half, left))
        full[0] = lax.dynamic_update_slice(full[0], other[j - 1], (start + (1 - core) * half, left))
    return None


def shared_bits():
    bits = bits_of(lax.axis_size("ctx"))
    return bits[1:-1] + bits[:1]


def near_count(block):
    return -(-(LONGEST - 1) // block)


def slot_blocks(block):
    n = lax.axis_size("ctx")
    half = n // 2
    ctx = lax.axis_index("ctx")
    places = [((ctx % half) ^ d, True) for d in held_of(shared_bits())]
    count = near_count(block)
    return places + [(ctx - d, ctx - d >= half) for d in list(range(1, count + 1)) + [0]]


def keys_back_flow(shared, near):
    n = lax.axis_size("ctx")
    half = n // 2
    block = shared.shape[0] // half
    count = near_count(block)
    held = shared
    for b in reversed(shared_bits()):
        m = held.shape[0] // 2
        got = yield [(held[m:], cswap(b))]
        held = plus(held[:m], got[0]).astype(bf16)
    got = yield [(held, move((c + half, c) for c in range(half)))] + [
        (near[(d - 1) * block : d * block], move((c, c - d) for c in range(half + d, n))) for d in range(1, count + 1)
    ]
    prompt = plus(held, got[0])
    own = near[count * block :].astype(f32)
    for arrived in got[1:]:
        own = own + arrived.astype(f32)
    return jnp.where(lax.axis_index("ctx") < half, prompt, own).astype(bf16)


def core_flow(value, axis):
    size = value.shape[axis] // 2
    mine = (lax.axis_index("ctx") % 2) * size
    keep = lax.dynamic_slice_in_dim(value, mine, size, axis=axis)
    send = lax.dynamic_slice_in_dim(value, size - mine, size, axis=axis)
    got = yield [(send, cswap(1))]
    return plus(keep, got[0]).astype(bf16)


def rows_flow(partial):
    planes = plane()
    me = lax.axis_index("fsdp")
    shard, cols = partial.shape[0] // planes, partial.shape[1]
    p = yield from core_flow(partial.reshape(planes, shard, cols), 1)
    p = p.reshape(2 * planes, shard // 4, cols)
    p = joined([rows(p, (me ^ j) * 2 + n // planes, 1)[0] for n, j in enumerate(order())])
    s = yield from scatter_flow(p)
    return s.astype(bf16)


def cores_flow(half, widths):
    core = lax.axis_index("ctx") % 2
    count = half.shape[0]
    (other,) = yield [(half, cswap(1))]
    outs, left = [], 0
    for width in widths:
        out = blank(2 * count, width, f32, outs[-1] if outs else other)
        for source, start in ((half, core * count), (other, (1 - core) * count)):
            out = put_rows(out, source[:, left : left + width].astype(f32), start)
        outs.append(out)
        left += width
    return outs


def direct_flow(value, widths):
    chips = lax.axis_size("ctx") // 2
    place = lax.axis_index("ctx") // 2
    size = value.shape[0] // chips
    others = range(1, chips)
    got = yield [(rows(value, (place ^ d) * size, size), cswap(2 * d)) for d in others]
    own = rows(value, place * size, size).astype(f32)
    for arrived in got:
        own = own + arrived.astype(f32)
    own = own.astype(bf16)
    got = yield [(own, cswap(2 * d)) for d in others]
    half = put_rows(blank(value.shape[0], value.shape[1], bf16, got[0]), own, place * size)
    for d, arrived in zip(others, got):
        half = put_rows(half, arrived, (place ^ d) * size)
    return (yield from cores_flow(half, widths))


def exchange_flow(own, stack):
    planes, size, cols = own.shape
    me = lax.axis_index("fsdp")
    pieces = [lax.dynamic_index_in_dim(own, me ^ j, 0, keepdims=False) for j in range(planes)]
    got = yield [(pieces[j], fswap(j)) for j in range(1, planes)]
    line = blank(size, planes * cols, bf16, got[0])
    width = cols // stack
    for j, piece in enumerate(pieces[:1] + got):
        for n in range(stack):
            part = piece[:, n * width : (n + 1) * width]
            line = lax.dynamic_update_slice(line, part, (0, n * planes * width + (me ^ j) * width))
    return line


def total_flow(value):
    for fn in [cswap(b) for b in bits_of(lax.axis_size("ctx"))] + [fswap(b) for b in bits_of(plane())]:
        got = yield [(value, fn)]
        value = value + got[0]
    return value


def local(
    hidden_in,
    cotangent,
    segment_ids,
    w_query,
    w_key,
    w_value,
    w_output,
    w_gate,
    w_up,
    w_down,
    attn_gain,
    ffn_gain,
):
    batches, block, width = hidden_in.shape
    tokens = segment_ids.shape[1]
    ctx = lax.axis_index("ctx")
    planes = plane()
    me = lax.axis_index("fsdp")
    first_row = ctx * block
    qd = w_query.shape[1]
    kvd = w_key.shape[1]
    shard = w_query.shape[0]
    ff_own = w_down.shape[0]
    groups = range(batches)

    line = Line()
    keys_weight = Flow(weight_flow(jnp.concatenate([w_key, w_value], axis=1)))
    query_weight = Flow(weight_flow(w_query))
    out_weight = Flow(weight_flow(w_output))
    gate_up = [blank(width, 2 * ff_own, bf16, w_gate)]
    gate_weight = Flow(column_flow(w_gate, gate_up, 0))
    up_weight = Flow(column_flow(w_up, gate_up, ff_own))
    gz = [Flow(gather_flow(cotangent[m])) for m in groups]

    line.launch(keys_weight)
    gains_own = jnp.stack([attn_gain, ffn_gain])
    gains = jnp.zeros((2, width), bf16)
    for j in range(planes):
        piece = fswap(j)(gains_own) if j else gains_own
        gains = lax.dynamic_update_slice(gains, piece, (0, (me ^ j) * shard))
    gains = gains.astype(f32)
    gain_attn, gain_ffn = gains[0], gains[1]
    segment_ids = line.settle(segment_ids)
    segments_later = segment_ids

    line.launch(keys_weight)
    hidden = hidden_in.reshape(batches * block, width).astype(f32)
    normed_attn, scaled_attn, inverse_attn = norm_parts(hidden, gain_attn)
    attn_in = normed_attn.astype(bf16)
    tables = [rotary_tables(positions_of(segment_ids[m], first_row, block)) for m in groups]
    cosine = joined([t[0] for t in tables])
    sine = joined([t[1] for t in tables])
    line.settle()

    line.launch(keys_weight, query_weight)
    line.settle()
    line.finish(keys_weight)
    line.launch(query_weight, out_weight)
    kv_own = project(attn_in, keys_weight.result, cosine, sine, False)
    kv_own, segments_later = line.settle(kv_own, segments_later + 0)
    keys = [lax.all_gather(kv_own[m * block : (m + 1) * block], "ctx", axis=0, tiled=True) for m in groups]
    line.launch(query_weight, out_weight, *gz)
    line.settle()
    line.finish(query_weight)
    line.launch(out_weight, gate_weight)
    queries = project(attn_in, query_weight.result, cosine, sine, True)

    slots = slot_blocks(block)
    places = jnp.stack([jnp.where(counts, p, 0) for p, counts in slots])
    after_all = jnp.stack([jnp.where(counts, 0, tokens) for _, counts in slots])
    within = jnp.arange(block, dtype=i32)
    query_index = first_row + within
    key_index = (places[:, None] * block + after_all[:, None] + within[None, :]).reshape(-1)
    biases, flags = [], []
    for m in groups:
        segments = segments_later[m]
        query_segments = lax.dynamic_slice_in_dim(segments, first_row, block)
        chosen = (places[:, None] == jnp.arange(tokens // block, dtype=i32)[None, :]).astype(i32)
        key_segments = jnp.sum(chosen[:, :, None] * segments.reshape(1, -1, block), axis=1).reshape(-1)
        visible = (key_index[:, None] <= query_index[None, :]) & (
            (key_segments[:, None] == query_segments[None, :]) | (key_segments[:, None] == 0)
        )
        biases.append(jnp.where(visible, 0.0, mask_fill).astype(f32))
        flags.append(jnp.any(visible.reshape(-1, block * block), axis=1).astype(i32))

    mixed, lses, middles, normed, b_flows = [], [], [], [], []

    def attention(m):
        o, lse = line.settle(*attend(flags[m], places, biases[m], queries, keys[m], m, block))
        mixed.append(o)
        lses.append(lse)

    def to_feed_forward(m):
        middle = hidden[m * block : (m + 1) * block] + nn(mixed[m], out_weight.result)
        normed_ffn, scaled, inverse = norm_parts(middle, gain_ffn)
        middles.append(middle)
        normed.append((scaled, inverse))
        b_flows.append(Flow(gather_flow(normed_ffn.astype(bf16))))

    attention(0)
    line.finish(out_weight)
    line.launch(gate_weight, up_weight, *gz)
    to_feed_forward(0)
    for m in groups[1:]:
        attention(m)
        line.launch(*b_flows, up_weight)
        to_feed_forward(m)
    line.settle()
    line.launch(*b_flows)
    line.settle()

    wide, out_parts, grad_flows, b_all = (), [], [], []
    line.finish(gate_weight, up_weight)
    for m in groups:
        line.finish(b_flows[m], gz[m])
        line.launch(*b_flows, *grad_flows)
        b = b_flows[m].result
        b_all.append(b)
        *wide, out_part, grad_part = feed_forward(b, gz[m].result[None], gate_up[0], w_down, m, batches, tuple(wide))
        out_part, grad_part = line.settle(out_part, grad_part)
        out_parts.append(Flow(scatter_flow(out_part), True))
        grad_flows.append(Flow(scatter_flow(grad_part), True))
    act, grad_wide = wide

    line.launch(*grad_flows)
    down = line.settle(product(act, joined([f.result for f in gz])))
    down_part = lax.psum_scatter(down, "ctx", scatter_dimension=0, tiled=True)
    line.launch(*grad_flows)
    line.settle()
    line.finish(*grad_flows)

    grad_middles, gys, grads_mixed = [], [], []
    grad_ffn_gain = jnp.zeros((width,), f32)
    for m in groups:
        scaled, inverse = normed[m]
        grad_part, gain_part = norm_back(grad_flows[m].result, middles[m], scaled, inverse, gain_ffn)
        grad_ffn_gain = grad_ffn_gain + gain_part
        grad_middle = cotangent[m].astype(f32) + grad_part
        gy = grad_middle.astype(bf16)
        grads_mixed.append(nt(gy, out_weight.result).astype(bf16))
        grad_middles.append(grad_middle)
        gys.append(gy)
    key_backs, grads_q = [], []
    for m in groups:
        line.launch(*key_backs)
        gq, *gkv = attend_back(
            flags[m], places, biases[m], queries, keys[m], mixed[m], grads_mixed[m], lses[m], cosine, sine, m, block
        )
        if m == 0:
            gq, *gkv, grads_mixed[-1], down_part = line.settle(gq, *gkv, grads_mixed[-1], down_part)
        else:
            gq, *gkv = line.settle(gq, *gkv)
        grads_q.append(gq)
        key_backs.append(Flow(keys_back_flow(*gkv), True))
    down_all = lax.all_gather(down_part, "ctx", axis=0, tiled=True)

    gq = joined(grads_q)
    line.launch(*key_backs)
    grad_up, down_all = line.settle(product(joined(b_all), grad_wide), down_all)
    up_part = lax.psum_scatter(
        grad_up.reshape(planes, shard, 2 * ff_own), "ctx", scatter_dimension=1, tiled=True
    )
    line.launch(*key_backs)
    grad_attn = line.settle(product(jnp.stack([attn_in, joined(mixed)]), jnp.stack([gq, joined(gys)])))
    grad_attn = Flow(rows_flow(grad_attn), True)
    line.launch(*key_backs, grad_attn)
    line.settle()
    line.finish(*key_backs)
    line.launch(grad_attn)
    gkv = unturn(joined([f.result for f in key_backs]), cosine, sine)
    grad_keys, gkv = line.settle(product(attn_in, gkv), gkv)
    grad_keys = Flow(rows_flow(grad_keys), True)
    line.launch(grad_attn, grad_keys)
    grad_attn_in = nt(gq, query_weight.result) + nt(gkv, keys_weight.result)
    grad_part, grad_attn_gain = norm_back(grad_attn_in, hidden, scaled_attn, inverse_attn, gain_attn)
    grad_in = (joined(grad_middles) + grad_part).astype(bf16)
    gains_back = Flow(total_flow(line.settle(jnp.stack([grad_attn_gain, grad_ffn_gain]))))
    line.finish(grad_attn)
    attn_out = Flow(direct_flow(grad_attn.result, [qd, width]))
    line.launch(attn_out, grad_keys, gains_back)
    line.settle()
    line.launch(attn_out, grad_keys, gains_back)
    up_part = line.settle(up_part)
    line.finish(grad_keys)
    keys_out = Flow(direct_flow(grad_keys.result, [kvd, kvd]))
    up_line = Flow(exchange_flow(up_part, 2))
    line.launch(up_line, attn_out, keys_out, gains_back)
    line.settle()
    line.finish(up_line)
    up_all = lax.all_gather(up_line.result, "ctx", axis=0, tiled=True)
    line.launch(keys_out, gains_back, *out_parts)
    line.settle()
    line.launch(keys_out, gains_back, *out_parts)
    up_all = line.settle(up_all)
    line.finish(attn_out, keys_out, gains_back, *out_parts)
    gain_grads = lax.dynamic_slice(gains_back.result, (0, me * shard), (2, shard))
    outputs = [(middles[m] + out_parts[m].result).astype(bf16) for m in groups]
    return (
        jnp.stack(outputs),
        grad_in.reshape(batches, block, width),
        attn_out.result[0],
        keys_out.result[0],
        keys_out.result[1],
        attn_out.result[1],
        up_all[:, : planes * ff_own].astype(f32),
        up_all[:, planes * ff_own :].astype(f32),
        down_all.astype(f32),
        gain_grads[0],
        gain_grads[1],
    )


def solution(mesh):
    tokens3 = P("fsdp", "ctx", None)
    matrix = P("fsdp", None)
    return jax.shard_map(
        local,
        mesh=mesh,
        in_specs=(tokens3, tokens3) + (matrix,) * 8 + (P("fsdp"),) * 2,
        out_specs=(tokens3, tokens3) + (matrix,) * 7 + (P("fsdp"),) * 2,
        check_vma=False,
    )
```

```python
import functools
import math

import jax
import jax.numpy as jnp
from jax import lax
from jax.experimental import pallas as pl
from jax.experimental.pallas import tpu as pltpu
from jax.sharding import PartitionSpec as P

HD = 128
PROMPT = 1024
CONT = 8
LONGEST = 192

eps_norm = 1e-05
rope_base = 1000000.0
mask_fill = -1e30
log2_e = 1.4426950408889634
bf16 = jnp.bfloat16
f32 = jnp.float32
i32 = jnp.int32
MIB = 1024 * 1024
SMALL = pl.CostEstimate(flops=0, bytes_accessed=0, transcendentals=0)


def positions_of(segments, first_row, block):
    own = lax.dynamic_slice_in_dim(segments, first_row, block)
    leading = jnp.sum((segments[None, :] < own[:, None]).astype(i32), axis=1)
    index = first_row + jnp.arange(block, dtype=i32)
    return jnp.where(own > 0, index - leading + PROMPT, index)


def rotary_tables(positions):
    half_width = HD // 2
    frequency = rope_base ** (-(jnp.arange(half_width, dtype=f32) * 2.0) / HD)
    angles = positions.astype(f32)[:, None] * frequency[None, :]
    cosine, sine = jnp.cos(angles), jnp.sin(angles)
    return (
        jnp.concatenate([cosine, cosine], axis=1),
        jnp.concatenate([-sine, sine], axis=1),
    )


def norm_parts(values, gain):
    inverse = lax.rsqrt(jnp.mean(values * values, axis=-1, keepdims=True) + eps_norm)
    scaled = values * inverse
    return (scaled * gain, scaled, inverse)


def norm_back(grad_out, values, scaled, inverse, gain):
    grad_scaled = grad_out * gain
    grad_gain = jnp.sum(grad_out * scaled, axis=0)
    along = jnp.mean(grad_scaled * values, axis=-1, keepdims=True)
    grad_values = inverse * grad_scaled - values * inverse * inverse * inverse * along
    return (grad_values, grad_gain)


def dot(left, right, dims, out=f32):
    return lax.dot_general(left, right, (dims, ((), ())), preferred_element_type=out)


def nn(left, right, out=f32):
    return dot(left, right, ((1,), (0,)), out)


def nt(left, right, out=f32):
    return dot(left, right, ((1,), (1,)), out)


def tn(left, right, out=f32):
    return dot(left, right, ((0,), (0,)), out)


def product_kernel(left_ref, right_ref, o_ref):
    o_ref[...] = tn(left_ref[0], right_ref[0]).astype(bf16)


def product(left, right):
    left = left[None] if left.ndim == 2 else left
    right = right[None] if right.ndim == 2 else right
    lefts, depth, count = left.shape
    stack, _, cols = right.shape
    side = min(count, cols, 1024)
    across = cols // side
    return pl.pallas_call(
        product_kernel,
        out_shape=jax.ShapeDtypeStruct((count, stack * cols), bf16),
        grid=(stack, count // side, across),
        in_specs=[
            pl.BlockSpec((1, depth, side), lambda n, i, j: (n % lefts, 0, i)),
            pl.BlockSpec((1, depth, side), lambda n, i, j: (n, 0, j)),
        ],
        out_specs=pl.BlockSpec((side, side), lambda n, i, j: (i, n * across + j)),
        compiler_params=pltpu.CompilerParams(vmem_limit_bytes=48 * MIB),
        cost_estimate=SMALL,
    )(left, right)


def turned(u, cosine, sine):
    return u * cosine + pltpu.roll(u, HD // 2, 1) * sine


def project_kernel(x_ref, first_ref, last_ref, cos_ref, sin_ref, o_ref, *, second):
    acc = nn(x_ref[...], jnp.concatenate([first_ref[...], last_ref[...]], axis=1))
    cosine, sine = cos_ref[...], sin_ref[...]
    o_ref[:, :HD] = turned(acc[:, :HD], cosine, sine).astype(bf16)
    last = acc[:, HD:]
    if second:
        last = turned(last, cosine, sine)
    o_ref[:, HD:] = last.astype(bf16)


def project(x, weight, cosine, sine, second):
    count, depth = x.shape
    cols = weight.shape[1]
    steps = cols // (2 * HD)
    whole = lambda i: (0, 0)
    first = (lambda i: (0, 2 * i)) if second else (lambda i: (0, i))
    last = (lambda i: (0, 2 * i + 1)) if second else (lambda i: (0, i + steps))
    return pl.pallas_call(
        functools.partial(project_kernel, second=second),
        out_shape=jax.ShapeDtypeStruct((count, cols), bf16),
        grid=(steps,),
        in_specs=[
            pl.BlockSpec((count, depth), whole),
            pl.BlockSpec((depth, HD), first),
            pl.BlockSpec((depth, HD), last),
            pl.BlockSpec((count, HD), whole),
            pl.BlockSpec((count, HD), whole),
        ],
        out_specs=pl.BlockSpec((count, 2 * HD), lambda i: (0, i)),
        compiler_params=pltpu.CompilerParams(vmem_limit_bytes=32 * MIB),
        cost_estimate=SMALL,
    )(x, weight, weight, cosine, sine)


def unturn_kernel(x_ref, cos_ref, sin_ref, o_ref):
    keys = pl.program_id(0) < pl.num_programs(0) // 2

    @pl.when(keys)
    def _():
        o_ref[...] = turned(x_ref[...].astype(f32), cos_ref[...], -sin_ref[...]).astype(bf16)

    @pl.when(jnp.logical_not(keys))
    def _():
        o_ref[...] = x_ref[...]


def unturn(x, cosine, sine):
    count, cols = x.shape
    heads = cols // (2 * HD)
    whole = lambda i: (0, 0)
    return pl.pallas_call(
        unturn_kernel,
        out_shape=jax.ShapeDtypeStruct((count, cols), bf16),
        grid=(2 * heads,),
        in_specs=[
            pl.BlockSpec((count, HD), lambda i: (0, jnp.where(i < heads, 2 * i, 2 * (i - heads) + 1))),
            pl.BlockSpec((count, HD), whole),
            pl.BlockSpec((count, HD), whole),
        ],
        out_specs=pl.BlockSpec((count, HD), lambda i: (0, i)),
    )(x, cosine, sine)


def stacked(ref):
    return jnp.concatenate([ref[:, :HD], ref[:, HD:]], axis=0)


def scores_of(keys, bias, queries):
    s = nt(keys, queries) * (log2_e / math.sqrt(HD))
    return s + jnp.concatenate([bias, bias], axis=1)


def key_rows(places, n, block):
    return pl.ds(pl.multiple_of(places[n] * block, block), block)


def attend_kernel(flags, places, bias_ref, q_ref, kv_ref, o_ref, lse_ref, m_ref, l_ref, acc_ref):
    queries = stacked(q_ref)
    block = q_ref.shape[0]
    m_ref[...] = jnp.full_like(m_ref, mask_fill)
    l_ref[...] = jnp.zeros_like(l_ref)
    acc_ref[...] = jnp.zeros_like(acc_ref)
    for n in range(bias_ref.shape[0] // block):

        @pl.when(flags[n] > 0)
        def _():
            at = key_rows(places, n, block)
            s = scores_of(kv_ref[at, :HD], bias_ref[n * block : (n + 1) * block, :], queries)
            m_old = m_ref[...]
            m_new = jnp.maximum(m_old, jnp.max(s, axis=0, keepdims=True))
            p = jnp.exp2(s - m_new)
            alpha = jnp.exp2(m_old - m_new)
            l_ref[...] = l_ref[...] * alpha + jnp.sum(p, axis=0, keepdims=True)
            acc_ref[...] = acc_ref[...] * alpha + tn(kv_ref[at, HD:], p.astype(bf16))
            m_ref[...] = m_new

    total = l_ref[...]
    out = (acc_ref[...] / total).T.astype(bf16)
    o_ref[:, :HD] = out[:block]
    o_ref[:, HD:] = out[block:]
    lse_ref[0] = m_ref[...] + jnp.log(total) * log2_e


def attend(flags, places, bias, queries, kv, m, block):
    tokens, cols = kv.shape
    heads = cols // (2 * HD)
    keys = bias.shape[0]
    return pl.pallas_call(
        attend_kernel,
        out_shape=(
            jax.ShapeDtypeStruct((block, cols), bf16),
            jax.ShapeDtypeStruct((heads, 1, 2 * block), f32),
        ),
        grid=(heads,),
        in_specs=[
            pl.BlockSpec(memory_space=pltpu.SMEM),
            pl.BlockSpec(memory_space=pltpu.SMEM),
            pl.BlockSpec((keys, block), lambda h: (0, 0)),
            pl.BlockSpec((block, 2 * HD), lambda h: (m, h)),
            pl.BlockSpec((tokens, 2 * HD), lambda h: (0, h)),
        ],
        out_specs=(
            pl.BlockSpec((block, 2 * HD), lambda h: (0, h)),
            pl.BlockSpec((1, 1, 2 * block), lambda h: (h, 0, 0)),
        ),
        scratch_shapes=[
            pltpu.VMEM((1, 2 * block), f32),
            pltpu.VMEM((1, 2 * block), f32),
            pltpu.VMEM((HD, 2 * block), f32),
        ],
        compiler_params=pltpu.CompilerParams(vmem_limit_bytes=32 * MIB),
        cost_estimate=SMALL,
    )(flags, places, bias, queries, kv)


def attend_back_kernel(
    flags,
    places,
    bias_ref,
    q_ref,
    kv_ref,
    o_ref,
    go_ref,
    lse_ref,
    cos_ref,
    sin_ref,
    gq_ref,
    gshared_ref,
    gnear_ref,
    acc_ref,
):
    queries = stacked(q_ref)
    block = q_ref.shape[0]
    grads = stacked(go_ref)
    product = grads.astype(f32) * stacked(o_ref).astype(f32)
    delta = jnp.sum(product.T, axis=0, keepdims=True)
    lse = lse_ref[0]
    acc_ref[...] = jnp.zeros_like(acc_ref)
    scale = 1.0 / math.sqrt(HD)
    for n in range(bias_ref.shape[0] // block):
        shared = gshared_ref.shape[0] // block
        to_ref, k = (gshared_ref, n) if n < shared else (gnear_ref, n - shared)
        to = slice(k * block, (k + 1) * block)

        @pl.when(flags[n] > 0)
        def _():
            at = key_rows(places, n, block)
            p = jnp.exp2(scores_of(kv_ref[at, :HD], bias_ref[n * block : (n + 1) * block, :], queries) - lse)
            gp = nt(kv_ref[at, HD:], grads)
            gs = (p * (gp - delta)).astype(bf16)
            acc_ref[...] += tn(kv_ref[at, :HD], gs)
            to_ref[to, :HD] = (nn(gs, queries) * scale).astype(bf16)
            to_ref[to, HD:] = nn(p.astype(bf16), grads).astype(bf16)

        @pl.when(flags[n] == 0)
        def _():
            to_ref[to, :] = jnp.zeros((block, 2 * HD), bf16)

    out = acc_ref[...].T * scale
    cosine, sine = cos_ref[...], -sin_ref[...]
    gq_ref[:, :HD] = turned(out[:block], cosine, sine).astype(bf16)
    gq_ref[:, HD:] = turned(out[block:], cosine, sine).astype(bf16)


def attend_back(flags, places, bias, queries, kv, mixed, grad_mixed, lse, cosine, sine, m, block):
    tokens, cols = kv.shape
    heads = cols // (2 * HD)
    keys = bias.shape[0]
    near = (near_count(block) + 1) * block
    own = pl.BlockSpec((block, 2 * HD), lambda h: (0, h))
    far = pl.BlockSpec((keys - near, 2 * HD), lambda h: (0, h))
    close = pl.BlockSpec((near, 2 * HD), lambda h: (0, h))
    return pl.pallas_call(
        attend_back_kernel,
        out_shape=(
            jax.ShapeDtypeStruct((block, cols), bf16),
            jax.ShapeDtypeStruct((keys - near, cols), bf16),
            jax.ShapeDtypeStruct((near, cols), bf16),
        ),
        grid=(heads,),
        in_specs=[
            pl.BlockSpec(memory_space=pltpu.SMEM),
            pl.BlockSpec(memory_space=pltpu.SMEM),
            pl.BlockSpec((keys, block), lambda h: (0, 0)),
            pl.BlockSpec((block, 2 * HD), lambda h: (m, h)),
            pl.BlockSpec((tokens, 2 * HD), lambda h: (0, h)),
            own,
            own,
            pl.BlockSpec((1, 1, 2 * block), lambda h: (h, 0, 0)),
            pl.BlockSpec((block, HD), lambda h: (m, 0)),
            pl.BlockSpec((block, HD), lambda h: (m, 0)),
        ],
        out_specs=(own, far, close),
        scratch_shapes=[pltpu.VMEM((HD, 2 * block), f32)],
        compiler_params=pltpu.CompilerParams(vmem_limit_bytes=40 * MIB),
        cost_estimate=SMALL,
    )(flags, places, bias, queries, kv, mixed, grad_mixed, lse, cosine, sine)


FCOLS = 256
FROWS = 512


def ffn_kernel(b_ref, gz_ref, wg_ref, wu_ref, wd_ref, act_ref, grads_ref, y_ref, gb_ref, yacc, gacc):
    step = pl.program_id(0)
    last = pl.num_programs(0) - 1

    @pl.when(step == 0)
    def _():
        yacc[...] = jnp.zeros_like(yacc)
        gacc[...] = jnp.zeros_like(gacc)

    def body(i, carry):
        at = pl.ds(pl.multiple_of(i * FROWS, FROWS), FROWS)
        w = jnp.concatenate([wg_ref[...], wu_ref[...]], axis=1)
        both = nn(b_ref[at, :], w)
        gate, up = both[:, :FCOLS], both[:, FCOLS:]
        grad_act = nt(gz_ref[0, at, :], wd_ref[...])
        sigma = jax.nn.sigmoid(gate)
        swish = gate * sigma
        act = (swish * up).astype(bf16)
        grad_gate = (grad_act * up * sigma * (1.0 + gate * (1.0 - sigma))).astype(bf16)
        grad_up = (grad_act * swish).astype(bf16)
        act_ref[at, :] = act
        grads_ref[0, at, :] = grad_gate
        grads_ref[1, at, :] = grad_up
        yacc[at, :] += nn(act, wd_ref[...])
        gacc[at, :] += nt(jnp.concatenate([grad_gate, grad_up], axis=1), w)
        return carry

    lax.fori_loop(0, b_ref.shape[0] // FROWS, body, 0)

    @pl.when(step == last)
    def _():
        y_ref[...] = yacc[...].astype(bf16)
        gb_ref[...] = gacc[...].astype(bf16)


def feed_forward(b, gz, gate_up, down, m, batches, kept):
    count, width = b.shape
    cols = down.shape[0]
    steps = cols // FCOLS
    once = pl.Buffered(1)
    wide = jax.ShapeDtypeStruct((batches * count, cols), bf16)
    narrow = jax.ShapeDtypeStruct((count, width), bf16)
    tile = pl.BlockSpec((count, FCOLS), lambda j: (m, j))
    total = pl.BlockSpec((count, width), lambda j: (0, 0), pipeline_mode=once)

    def kernel(*refs):
        ffn_kernel(*refs[:5], *refs[5 + len(kept) :])

    return pl.pallas_call(
        kernel,
        out_shape=(wide, jax.ShapeDtypeStruct((2,) + wide.shape, bf16), narrow, narrow),
        grid=(steps,),
        in_specs=[
            pl.BlockSpec((count, width), lambda j: (0, 0), pipeline_mode=once),
            pl.BlockSpec((1, count, width), lambda j: (0, 0, 0), pipeline_mode=once),
            pl.BlockSpec((width, FCOLS), lambda j: (0, j)),
            pl.BlockSpec((width, FCOLS), lambda j: (0, j + steps)),
            pl.BlockSpec((FCOLS, width), lambda j: (j, 0)),
        ]
        + [pl.BlockSpec(memory_space=pl.ANY)] * len(kept),
        out_specs=(tile, pl.BlockSpec((2, count, FCOLS), lambda j: (0, m, j)), total, total),
        scratch_shapes=[pltpu.VMEM((count, width), f32), pltpu.VMEM((count, width), f32)],
        input_output_aliases={5 + i: i for i in range(len(kept))},
        compiler_params=pltpu.CompilerParams(vmem_limit_bytes=60 * MIB),
        cost_estimate=SMALL,
    )(b, gz, gate_up, gate_up, down, *kept)


def plane():
    return lax.axis_size("fsdp")


def bits_of(n):
    return [1 << i for i in range(n.bit_length() - 1)]


def fswap(bits):
    return lambda value: lax.ppermute(value, "fsdp", [(i, i ^ bits) for i in range(plane())])


def cswap(bits):
    return lambda value: lax.ppermute(value, "ctx", [(i, i ^ bits) for i in range(lax.axis_size("ctx"))])


def move(pairs):
    pairs = list(pairs)
    return lambda value: lax.ppermute(value, "ctx", pairs)


def rows(value, start, size):
    return lax.dynamic_slice_in_dim(value, start, size, axis=0)


def put_rows(target, value, start):
    return lax.dynamic_update_slice_in_dim(target, value, start, axis=0)


def plus(left, right):
    return left.astype(f32) + right.astype(f32)


def joined(parts):
    return jnp.concatenate(parts, axis=0) if len(parts) > 1 else parts[0]


def blank(rows_count, cols, kind, source):
    anywhere = pl.BlockSpec(memory_space=pl.ANY)
    return pl.pallas_call(
        lambda source_ref, out_ref: None,
        out_shape=jax.ShapeDtypeStruct((rows_count, cols), kind),
        in_specs=[anywhere],
        out_specs=anywhere,
    )(source)


def gate(values):
    if len(values) < 2:
        return list(values)
    anywhere = pl.BlockSpec(memory_space=pl.ANY)
    out = pl.pallas_call(
        lambda *refs: None,
        out_shape=[jax.ShapeDtypeStruct(v.shape, v.dtype) for v in values],
        in_specs=[anywhere] * len(values),
        out_specs=[anywhere] * len(values),
        input_output_aliases={i: i for i in range(len(values))},
        cost_estimate=SMALL,
    )(*values)
    return list(out)


class Flow:
    def __init__(self, steps, fresh=False):
        self.steps, self.result, self.want, self.got = steps, None, [], None
        self.fresh = fresh
        self.go(None)

    def go(self, given):
        try:
            self.want = self.steps.send(given)
        except StopIteration as stop:
            self.want, self.result = [], stop.value


class Line:
    def __init__(self):
        self.under_way = []

    def launch(self, *flows):
        flows = [f for f in flows if f.want]
        ready = gate([value for f in flows if f.fresh for value, _ in f.want])
        for f in flows:
            f.got = [fn(ready.pop(0) if f.fresh else value) for value, fn in f.want]
            self.under_way.append(f)

    def settle(self, *held):
        gated = gate([a for f in self.under_way for a in f.got] + list(held))
        for f in self.under_way:
            given, gated = gated[: len(f.got)], gated[len(f.got) :]
            f.go(given)
        self.under_way = []
        return gated[0] if len(held) == 1 else gated

    def finish(self, *flows):
        if self.under_way:
            self.settle()
        while any(f.want for f in flows):
            self.launch(*flows)
            self.settle()


def order():
    out = []
    for bits in (bits_of(plane()), bits_of(plane())[::-1]):
        ds = [0]
        for b in bits:
            ds = ds + [d ^ b for d in ds]
        out += ds
    return out


def gather_flow(own):
    half = own.shape[0] // 2
    first, last = own[:half], own[half:]
    bits = bits_of(plane())
    for a, b in zip(bits, bits[::-1]):
        got = yield [(first, fswap(a)), (last, fswap(b))]
        first = joined([first, got[0]])
        last = joined([last, got[1]])
    return joined([first, last])


def scatter_flow(parts):
    total = parts.shape[0] // 2
    first, last = parts[:total], parts[total:]
    bits = bits_of(plane())
    for a, b in zip(bits[::-1], bits):
        n = first.shape[0] // 2
        got = yield [(first[n:].astype(bf16), fswap(a)), (last[n:].astype(bf16), fswap(b))]
        first = plus(first[:n], got[0])
        last = plus(last[:n], got[1])
    return joined([first, last])


def weight_flow(own):
    shard, cols = own.shape
    me = lax.axis_index("fsdp")
    core = lax.axis_index("ctx") % 2
    half, part = shard // 2, shard // 4
    full = None
    mine = rows(own, core * half, half)
    first, last = mine[:part], mine[part:]
    bits = bits_of(plane())
    held, pending = [0], []
    for a, b in zip(bits + [None], bits[::-1] + [None]):
        want = [(value, cswap(1)) for value, _, _ in pending]
        if a is not None:
            want += [(first, fswap(a)), (last, fswap(b))]
        got = yield want
        if full is None:
            full = put_rows(blank(shard * plane(), cols, bf16, got[0]), own, me * shard)
        for n, (here, ds, offset) in enumerate(pending):
            for k, d in enumerate(ds):
                at = slice(k * part, (k + 1) * part)
                start = (me ^ d) * shard + offset
                full = put_rows(full, here[at], start + core * half)
                full = put_rows(full, got[n][at], start + (1 - core) * half)
        if a is not None:
            order_a = held_of(bits[: bits.index(a)])
            order_b = held_of(bits[::-1][: bits[::-1].index(b)])
            n = len(pending)
            pending = [
                (got[n], [d ^ a for d in order_a], 0),
                (got[n + 1], [d ^ b for d in order_b], part),
            ]
            first = joined([first, got[n]])
            last = joined([last, got[n + 1]])
    return full


def held_of(bits):
    ds = [0]
    for b in bits:
        ds = ds + [d ^ b for d in ds]
    return ds


def column_flow(weights, full, left):
    me = lax.axis_index("fsdp")
    core = lax.axis_index("ctx") % 2
    planes = plane()
    shard = weights.shape[0]
    half = shard // 2
    size = weights.shape[1] // planes

    def columns(j, start, count):
        return lax.dynamic_slice(weights, (start, (me ^ j) * size), (count, size))

    got = yield [(columns(j, core * half, half), fswap(j)) for j in range(1, planes)]
    full[0] = lax.dynamic_update_slice(full[0], columns(0, 0, shard), (me * shard, left))
    other = yield [(piece, cswap(1)) for piece in got]
    for j in range(1, planes):
        start = (me ^ j) * shard
        full[0] = lax.dynamic_update_slice(full[0], got[j - 1], (start + core * half, left))
        full[0] = lax.dynamic_update_slice(full[0], other[j - 1], (start + (1 - core) * half, left))
    return None


def shared_bits():
    bits = bits_of(lax.axis_size("ctx"))
    return bits[1:-1] + bits[:1]


def near_count(block):
    return -(-(LONGEST - 1) // block)


def slot_blocks(block):
    n = lax.axis_size("ctx")
    half = n // 2
    ctx = lax.axis_index("ctx")
    places = [((ctx % half) ^ d, True) for d in held_of(shared_bits())]
    count = near_count(block)
    return places + [(ctx - d, ctx - d >= half) for d in list(range(1, count + 1)) + [0]]


def keys_back_flow(shared, near):
    n = lax.axis_size("ctx")
    half = n // 2
    block = shared.shape[0] // half
    count = near_count(block)
    held = shared
    for b in reversed(shared_bits()):
        m = held.shape[0] // 2
        got = yield [(held[m:], cswap(b))]
        held = plus(held[:m], got[0]).astype(bf16)
    got = yield [(held, move((c + half, c) for c in range(half)))] + [
        (near[(d - 1) * block : d * block], move((c, c - d) for c in range(half + d, n))) for d in range(1, count + 1)
    ]
    prompt = plus(held, got[0])
    own = near[count * block :].astype(f32)
    for arrived in got[1:]:
        own = own + arrived.astype(f32)
    return jnp.where(lax.axis_index("ctx") < half, prompt, own).astype(bf16)


def core_flow(value, axis):
    size = value.shape[axis] // 2
    mine = (lax.axis_index("ctx") % 2) * size
    keep = lax.dynamic_slice_in_dim(value, mine, size, axis=axis)
    send = lax.dynamic_slice_in_dim(value, size - mine, size, axis=axis)
    got = yield [(send, cswap(1))]
    return plus(keep, got[0]).astype(bf16)


def rows_flow(partial):
    planes = plane()
    me = lax.axis_index("fsdp")
    shard, cols = partial.shape[0] // planes, partial.shape[1]
    p = yield from core_flow(partial.reshape(planes, shard, cols), 1)
    p = p.reshape(2 * planes, shard // 4, cols)
    p = joined([rows(p, (me ^ j) * 2 + n // planes, 1)[0] for n, j in enumerate(order())])
    s = yield from scatter_flow(p)
    return s.astype(bf16)


def cores_flow(half, widths):
    core = lax.axis_index("ctx") % 2
    count = half.shape[0]
    (other,) = yield [(half, cswap(1))]
    outs, left = [], 0
    for width in widths:
        out = blank(2 * count, width, f32, outs[-1] if outs else other)
        for source, start in ((half, core * count), (other, (1 - core) * count)):
            out = put_rows(out, source[:, left : left + width].astype(f32), start)
        outs.append(out)
        left += width
    return outs


def direct_flow(value, widths):
    chips = lax.axis_size("ctx") // 2
    place = lax.axis_index("ctx") // 2
    size = value.shape[0] // chips
    others = range(1, chips)
    got = yield [(rows(value, (place ^ d) * size, size), cswap(2 * d)) for d in others]
    own = rows(value, place * size, size).astype(f32)
    for arrived in got:
        own = own + arrived.astype(f32)
    own = own.astype(bf16)
    got = yield [(own, cswap(2 * d)) for d in others]
    half = put_rows(blank(value.shape[0], value.shape[1], bf16, got[0]), own, place * size)
    for d, arrived in zip(others, got):
        half = put_rows(half, arrived, (place ^ d) * size)
    return (yield from cores_flow(half, widths))


def exchange_flow(own, stack):
    planes, size, cols = own.shape
    me = lax.axis_index("fsdp")
    pieces = [lax.dynamic_index_in_dim(own, me ^ j, 0, keepdims=False) for j in range(planes)]
    got = yield [(pieces[j], fswap(j)) for j in range(1, planes)]
    line = blank(size, planes * cols, bf16, got[0])
    width = cols // stack
    for j, piece in enumerate(pieces[:1] + got):
        for n in range(stack):
            part = piece[:, n * width : (n + 1) * width]
            line = lax.dynamic_update_slice(line, part, (0, n * planes * width + (me ^ j) * width))
    return line


def total_flow(value):
    for fn in [cswap(b) for b in bits_of(lax.axis_size("ctx"))] + [fswap(b) for b in bits_of(plane())]:
        got = yield [(value, fn)]
        value = value + got[0]
    return value


def local(
    hidden_in,
    cotangent,
    segment_ids,
    w_query,
    w_key,
    w_value,
    w_output,
    w_gate,
    w_up,
    w_down,
    attn_gain,
    ffn_gain,
):
    batches, block, width = hidden_in.shape
    tokens = segment_ids.shape[1]
    ctx = lax.axis_index("ctx")
    planes = plane()
    me = lax.axis_index("fsdp")
    first_row = ctx * block
    qd = w_query.shape[1]
    kvd = w_key.shape[1]
    shard = w_query.shape[0]
    ff_own = w_down.shape[0]
    groups = range(batches)

    line = Line()
    keys_weight = Flow(weight_flow(jnp.concatenate([w_key, w_value], axis=1)))
    query_weight = Flow(weight_flow(w_query))
    out_weight = Flow(weight_flow(w_output))
    gate_up = [blank(width, 2 * ff_own, bf16, w_gate)]
    gate_weight = Flow(column_flow(w_gate, gate_up, 0))
    up_weight = Flow(column_flow(w_up, gate_up, ff_own))
    gz = [Flow(gather_flow(cotangent[m])) for m in groups]

    line.launch(keys_weight)
    gains_own = jnp.stack([attn_gain, ffn_gain])
    gains = jnp.zeros((2, width), bf16)
    for j in range(planes):
        piece = fswap(j)(gains_own) if j else gains_own
        gains = lax.dynamic_update_slice(gains, piece, (0, (me ^ j) * shard))
    gains = gains.astype(f32)
    gain_attn, gain_ffn = gains[0], gains[1]
    segment_ids = line.settle(segment_ids)
    segments_later = segment_ids

    line.launch(keys_weight)
    hidden = hidden_in.reshape(batches * block, width).astype(f32)
    normed_attn, scaled_attn, inverse_attn = norm_parts(hidden, gain_attn)
    attn_in = normed_attn.astype(bf16)
    tables = [rotary_tables(positions_of(segment_ids[m], first_row, block)) for m in groups]
    cosine = joined([t[0] for t in tables])
    sine = joined([t[1] for t in tables])
    line.settle()

    line.launch(keys_weight, query_weight)
    line.settle()
    line.finish(keys_weight)
    line.launch(query_weight, out_weight)
    kv_own = project(attn_in, keys_weight.result, cosine, sine, False)
    kv_own, segments_later = line.settle(kv_own, segments_later + 0)
    keys = [lax.all_gather(kv_own[m * block : (m + 1) * block], "ctx", axis=0, tiled=True) for m in groups]
    line.launch(query_weight, out_weight, *gz)
    line.settle()
    line.finish(query_weight)
    line.launch(out_weight, gate_weight)
    queries = project(attn_in, query_weight.result, cosine, sine, True)

    slots = slot_blocks(block)
    places = jnp.stack([jnp.where(counts, p, 0) for p, counts in slots])
    after_all = jnp.stack([jnp.where(counts, 0, tokens) for _, counts in slots])
    within = jnp.arange(block, dtype=i32)
    query_index = first_row + within
    key_index = (places[:, None] * block + after_all[:, None] + within[None, :]).reshape(-1)
    biases, flags = [], []
    for m in groups:
        segments = segments_later[m]
        query_segments = lax.dynamic_slice_in_dim(segments, first_row, block)
        chosen = (places[:, None] == jnp.arange(tokens // block, dtype=i32)[None, :]).astype(i32)
        key_segments = jnp.sum(chosen[:, :, None] * segments.reshape(1, -1, block), axis=1).reshape(-1)
        visible = (key_index[:, None] <= query_index[None, :]) & (
            (key_segments[:, None] == query_segments[None, :]) | (key_segments[:, None] == 0)
        )
        biases.append(jnp.where(visible, 0.0, mask_fill).astype(f32))
        flags.append(jnp.any(visible.reshape(-1, block * block), axis=1).astype(i32))

    mixed, lses, middles, normed, b_flows = [], [], [], [], []

    def attention(m):
        o, lse = line.settle(*attend(flags[m], places, biases[m], queries, keys[m], m, block))
        mixed.append(o)
        lses.append(lse)

    def to_feed_forward(m):
        middle = hidden[m * block : (m + 1) * block] + nn(mixed[m], out_weight.result)
        normed_ffn, scaled, inverse = norm_parts(middle, gain_ffn)
        middles.append(middle)
        normed.append((scaled, inverse))
        b_flows.append(Flow(gather_flow(normed_ffn.astype(bf16))))

    attention(0)
    line.finish(out_weight)
    line.launch(gate_weight, up_weight, *gz)
    to_feed_forward(0)
    for m in groups[1:]:
        attention(m)
        line.launch(*b_flows, up_weight)
        to_feed_forward(m)
    line.settle()
    line.launch(*b_flows)
    line.settle()

    wide, out_parts, grad_flows, b_all = (), [], [], []
    line.finish(gate_weight, up_weight)
    for m in groups:
        line.finish(b_flows[m], gz[m])
        line.launch(*b_flows, *grad_flows)
        b = b_flows[m].result
        b_all.append(b)
        *wide, out_part, grad_part = feed_forward(b, gz[m].result[None], gate_up[0], w_down, m, batches, tuple(wide))
        out_part, grad_part = line.settle(out_part, grad_part)
        out_parts.append(Flow(scatter_flow(out_part), True))
        grad_flows.append(Flow(scatter_flow(grad_part), True))
    act, grad_wide = wide

    line.launch(*grad_flows)
    grad_up = line.settle(product(joined(b_all), grad_wide))
    up_part = lax.psum_scatter(
        grad_up.reshape(planes, shard, 2 * ff_own), "ctx", scatter_dimension=1, tiled=True
    )
    line.launch(*grad_flows)
    line.settle()
    line.finish(*grad_flows)

    grad_middles, gys, grads_mixed = [], [], []
    grad_ffn_gain = jnp.zeros((width,), f32)
    for m in groups:
        scaled, inverse = normed[m]
        grad_part, gain_part = norm_back(grad_flows[m].result, middles[m], scaled, inverse, gain_ffn)
        grad_ffn_gain = grad_ffn_gain + gain_part
        grad_middle = cotangent[m].astype(f32) + grad_part
        gy = grad_middle.astype(bf16)
        grads_mixed.append(nt(gy, out_weight.result).astype(bf16))
        grad_middles.append(grad_middle)
        gys.append(gy)
    key_backs, grads_q = [], []
    for m in groups:
        line.launch(*key_backs)
        gq, *gkv = attend_back(
            flags[m], places, biases[m], queries, keys[m], mixed[m], grads_mixed[m], lses[m], cosine, sine, m, block
        )
        if m + 1 < batches:
            gq, *gkv, grads_mixed[-1] = line.settle(gq, *gkv, grads_mixed[-1])
        else:
            gq, *gkv = line.settle(gq, *gkv)
        grads_q.append(gq)
        key_backs.append(Flow(keys_back_flow(*gkv), True))

    gq = joined(grads_q)
    line.launch(*key_backs)
    grad_down = product(act, joined([f.result for f in gz]))
    grad_attn = product(jnp.stack([attn_in, joined(mixed)]), jnp.stack([gq, joined(gys)]))
    grad_down, grad_attn, up_part = line.settle(grad_down, grad_attn, up_part)
    down_part = lax.psum_scatter(grad_down, "ctx", scatter_dimension=0, tiled=True)
    grad_attn = Flow(rows_flow(grad_attn), True)
    up_line = Flow(exchange_flow(up_part, 2))
    line.launch(*key_backs, grad_attn, up_line)
    line.settle()
    line.finish(up_line)
    up_all = lax.all_gather(up_line.result, "ctx", axis=0, tiled=True)
    line.launch(*key_backs, grad_attn)
    line.settle()
    line.finish(*key_backs)
    line.launch(grad_attn)
    gkv = unturn(joined([f.result for f in key_backs]), cosine, sine)
    grad_keys, gkv, down_part = line.settle(product(attn_in, gkv), gkv, down_part)
    grad_keys = Flow(rows_flow(grad_keys), True)
    line.finish(grad_attn)
    line.launch(grad_keys)
    grad_attn_in = nt(gq, query_weight.result) + nt(gkv, keys_weight.result)
    grad_part, grad_attn_gain = norm_back(grad_attn_in, hidden, scaled_attn, inverse_attn, gain_attn)
    grad_in = (joined(grad_middles) + grad_part).astype(bf16)
    gain_grads, down_part = line.settle(jnp.stack([grad_attn_gain, grad_ffn_gain]), down_part)
    gains_back = Flow(total_flow(gain_grads))
    line.launch(grad_keys, gains_back)
    down_part = line.settle(down_part)
    down_all = lax.all_gather(down_part, "ctx", axis=0, tiled=True)
    line.launch(grad_keys, gains_back)
    line.settle()
    line.finish(grad_keys)
    both = jnp.concatenate([grad_attn.result, grad_keys.result], axis=1)
    attn_out = Flow(direct_flow(both, [qd, width, kvd, kvd]))
    line.launch(attn_out, gains_back)
    up_all = line.settle(up_all)
    grad_gate = up_all[:, : planes * ff_own].astype(f32)
    grad_up = up_all[:, planes * ff_own :].astype(f32)
    line.launch(attn_out, gains_back, *out_parts)
    grad_gate, grad_up, down_all = line.settle(grad_gate, grad_up, down_all)
    grad_down = down_all.astype(f32)
    line.launch(attn_out, gains_back, *out_parts)
    grad_down = line.settle(grad_down)
    line.finish(attn_out, gains_back, *out_parts)
    gain_grads = lax.dynamic_slice(gains_back.result, (0, me * shard), (2, shard))
    outputs = [(middles[m] + out_parts[m].result).astype(bf16) for m in groups]
    return (
        jnp.stack(outputs),
        grad_in.reshape(batches, block, width),
        attn_out.result[0],
        attn_out.result[2],
        attn_out.result[3],
        attn_out.result[1],
        grad_gate,
        grad_up,
        grad_down,
        gain_grads[0],
        gain_grads[1],
    )


def solution(mesh):
    tokens3 = P("fsdp", "ctx", None)
    matrix = P("fsdp", None)
    return jax.shard_map(
        local,
        mesh=mesh,
        in_specs=(tokens3, tokens3) + (matrix,) * 8 + (P("fsdp"),) * 2,
        out_specs=(tokens3, tokens3) + (matrix,) * 7 + (P("fsdp"),) * 2,
        check_vma=False,
    )
```

```python
import functools
import math

import jax
import jax.numpy as jnp
from jax import lax
from jax.experimental import pallas as pl
from jax.experimental.pallas import tpu as pltpu
from jax.sharding import PartitionSpec as P

HD = 128
PROMPT = 1024
CONT = 8
LONGEST = 192

eps_norm = 1e-05
rope_base = 1000000.0
mask_fill = -1e30
log2_e = 1.4426950408889634
bf16 = jnp.bfloat16
f32 = jnp.float32
i32 = jnp.int32
MIB = 1024 * 1024
SMALL = pl.CostEstimate(flops=0, bytes_accessed=0, transcendentals=0)


def positions_of(segments, first_row, block):
    own = lax.dynamic_slice_in_dim(segments, first_row, block)
    leading = jnp.sum((segments[None, :] < own[:, None]).astype(i32), axis=1)
    index = first_row + jnp.arange(block, dtype=i32)
    return jnp.where(own > 0, index - leading + PROMPT, index)


def rotary_tables(positions):
    half_width = HD // 2
    frequency = rope_base ** (-(jnp.arange(half_width, dtype=f32) * 2.0) / HD)
    angles = positions.astype(f32)[:, None] * frequency[None, :]
    cosine, sine = jnp.cos(angles), jnp.sin(angles)
    return (
        jnp.concatenate([cosine, cosine], axis=1),
        jnp.concatenate([-sine, sine], axis=1),
    )


def norm_parts(values, gain):
    inverse = lax.rsqrt(jnp.mean(values * values, axis=-1, keepdims=True) + eps_norm)
    scaled = values * inverse
    return (scaled * gain, scaled, inverse)


def norm_back(grad_out, values, scaled, inverse, gain):
    grad_scaled = grad_out * gain
    grad_gain = jnp.sum(grad_out * scaled, axis=0)
    along = jnp.mean(grad_scaled * values, axis=-1, keepdims=True)
    grad_values = inverse * grad_scaled - values * inverse * inverse * inverse * along
    return (grad_values, grad_gain)


def dot(left, right, dims, out=f32):
    return lax.dot_general(left, right, (dims, ((), ())), preferred_element_type=out)


def nn(left, right, out=f32):
    return dot(left, right, ((1,), (0,)), out)


def nt(left, right, out=f32):
    return dot(left, right, ((1,), (1,)), out)


def tn(left, right, out=f32):
    return dot(left, right, ((0,), (0,)), out)


def product_kernel(left_ref, right_ref, o_ref):
    o_ref[...] = tn(left_ref[0], right_ref[0]).astype(bf16)


def product(left, right):
    left = left[None] if left.ndim == 2 else left
    right = right[None] if right.ndim == 2 else right
    lefts, depth, count = left.shape
    stack, _, cols = right.shape
    side = min(count, cols, 1024)
    across = cols // side
    return pl.pallas_call(
        product_kernel,
        out_shape=jax.ShapeDtypeStruct((count, stack * cols), bf16),
        grid=(stack, count // side, across),
        in_specs=[
            pl.BlockSpec((1, depth, side), lambda n, i, j: (n % lefts, 0, i)),
            pl.BlockSpec((1, depth, side), lambda n, i, j: (n, 0, j)),
        ],
        out_specs=pl.BlockSpec((side, side), lambda n, i, j: (i, n * across + j)),
        compiler_params=pltpu.CompilerParams(vmem_limit_bytes=48 * MIB),
        cost_estimate=SMALL,
    )(left, right)


def turned(u, cosine, sine):
    return u * cosine + pltpu.roll(u, HD // 2, 1) * sine


def project_kernel(x_ref, first_ref, last_ref, cos_ref, sin_ref, o_ref, *, second):
    acc = nn(x_ref[...], jnp.concatenate([first_ref[...], last_ref[...]], axis=1))
    cosine, sine = cos_ref[...], sin_ref[...]
    o_ref[:, :HD] = turned(acc[:, :HD], cosine, sine).astype(bf16)
    last = acc[:, HD:]
    if second:
        last = turned(last, cosine, sine)
    o_ref[:, HD:] = last.astype(bf16)


def project(x, weight, cosine, sine, second):
    count, depth = x.shape
    cols = weight.shape[1]
    steps = cols // (2 * HD)
    whole = lambda i: (0, 0)
    first = (lambda i: (0, 2 * i)) if second else (lambda i: (0, i))
    last = (lambda i: (0, 2 * i + 1)) if second else (lambda i: (0, i + steps))
    return pl.pallas_call(
        functools.partial(project_kernel, second=second),
        out_shape=jax.ShapeDtypeStruct((count, cols), bf16),
        grid=(steps,),
        in_specs=[
            pl.BlockSpec((count, depth), whole),
            pl.BlockSpec((depth, HD), first),
            pl.BlockSpec((depth, HD), last),
            pl.BlockSpec((count, HD), whole),
            pl.BlockSpec((count, HD), whole),
        ],
        out_specs=pl.BlockSpec((count, 2 * HD), lambda i: (0, i)),
        compiler_params=pltpu.CompilerParams(vmem_limit_bytes=32 * MIB),
        cost_estimate=SMALL,
    )(x, weight, weight, cosine, sine)


def unturn_kernel(x_ref, cos_ref, sin_ref, o_ref):
    keys = pl.program_id(0) < pl.num_programs(0) // 2

    @pl.when(keys)
    def _():
        o_ref[...] = turned(x_ref[...].astype(f32), cos_ref[...], -sin_ref[...]).astype(bf16)

    @pl.when(jnp.logical_not(keys))
    def _():
        o_ref[...] = x_ref[...]


def unturn(x, cosine, sine):
    count, cols = x.shape
    heads = cols // (2 * HD)
    whole = lambda i: (0, 0)
    return pl.pallas_call(
        unturn_kernel,
        out_shape=jax.ShapeDtypeStruct((count, cols), bf16),
        grid=(2 * heads,),
        in_specs=[
            pl.BlockSpec((count, HD), lambda i: (0, jnp.where(i < heads, 2 * i, 2 * (i - heads) + 1))),
            pl.BlockSpec((count, HD), whole),
            pl.BlockSpec((count, HD), whole),
        ],
        out_specs=pl.BlockSpec((count, HD), lambda i: (0, i)),
    )(x, cosine, sine)


def stacked(ref):
    return jnp.concatenate([ref[:, :HD], ref[:, HD:]], axis=0)


def scores_of(keys, bias, queries):
    s = nt(keys, queries) * (log2_e / math.sqrt(HD))
    return s + jnp.concatenate([bias, bias], axis=1)


def key_rows(places, n, block):
    return pl.ds(pl.multiple_of(places[n] * block, block), block)


def attend_kernel(flags, places, bias_ref, q_ref, kv_ref, o_ref, lse_ref, m_ref, l_ref, acc_ref):
    queries = stacked(q_ref)
    block = q_ref.shape[0]
    m_ref[...] = jnp.full_like(m_ref, mask_fill)
    l_ref[...] = jnp.zeros_like(l_ref)
    acc_ref[...] = jnp.zeros_like(acc_ref)
    for n in range(bias_ref.shape[0] // block):

        @pl.when(flags[n] > 0)
        def _():
            at = key_rows(places, n, block)
            s = scores_of(kv_ref[at, :HD], bias_ref[n * block : (n + 1) * block, :], queries)
            m_old = m_ref[...]
            m_new = jnp.maximum(m_old, jnp.max(s, axis=0, keepdims=True))
            p = jnp.exp2(s - m_new)
            alpha = jnp.exp2(m_old - m_new)
            l_ref[...] = l_ref[...] * alpha + jnp.sum(p, axis=0, keepdims=True)
            acc_ref[...] = acc_ref[...] * alpha + tn(kv_ref[at, HD:], p.astype(bf16))
            m_ref[...] = m_new

    total = l_ref[...]
    out = (acc_ref[...] / total).T.astype(bf16)
    o_ref[:, :HD] = out[:block]
    o_ref[:, HD:] = out[block:]
    lse_ref[0] = m_ref[...] + jnp.log(total) * log2_e


def attend(flags, places, bias, queries, kv, m, block):
    tokens, cols = kv.shape
    heads = cols // (2 * HD)
    keys = bias.shape[0]
    return pl.pallas_call(
        attend_kernel,
        out_shape=(
            jax.ShapeDtypeStruct((block, cols), bf16),
            jax.ShapeDtypeStruct((heads, 1, 2 * block), f32),
        ),
        grid=(heads,),
        in_specs=[
            pl.BlockSpec(memory_space=pltpu.SMEM),
            pl.BlockSpec(memory_space=pltpu.SMEM),
            pl.BlockSpec((keys, block), lambda h: (0, 0)),
            pl.BlockSpec((block, 2 * HD), lambda h: (m, h)),
            pl.BlockSpec((tokens, 2 * HD), lambda h: (0, h)),
        ],
        out_specs=(
            pl.BlockSpec((block, 2 * HD), lambda h: (0, h)),
            pl.BlockSpec((1, 1, 2 * block), lambda h: (h, 0, 0)),
        ),
        scratch_shapes=[
            pltpu.VMEM((1, 2 * block), f32),
            pltpu.VMEM((1, 2 * block), f32),
            pltpu.VMEM((HD, 2 * block), f32),
        ],
        compiler_params=pltpu.CompilerParams(vmem_limit_bytes=32 * MIB),
        cost_estimate=SMALL,
    )(flags, places, bias, queries, kv)


def attend_back_kernel(
    flags,
    places,
    bias_ref,
    q_ref,
    kv_ref,
    o_ref,
    go_ref,
    lse_ref,
    cos_ref,
    sin_ref,
    gq_ref,
    gshared_ref,
    gnear_ref,
    acc_ref,
):
    queries = stacked(q_ref)
    block = q_ref.shape[0]
    grads = stacked(go_ref)
    product = grads.astype(f32) * stacked(o_ref).astype(f32)
    delta = jnp.sum(product.T, axis=0, keepdims=True)
    lse = lse_ref[0]
    acc_ref[...] = jnp.zeros_like(acc_ref)
    scale = 1.0 / math.sqrt(HD)
    for n in range(bias_ref.shape[0] // block):
        shared = gshared_ref.shape[0] // block
        to_ref, k = (gshared_ref, n) if n < shared else (gnear_ref, n - shared)
        to = slice(k * block, (k + 1) * block)

        @pl.when(flags[n] > 0)
        def _():
            at = key_rows(places, n, block)
            p = jnp.exp2(scores_of(kv_ref[at, :HD], bias_ref[n * block : (n + 1) * block, :], queries) - lse)
            gp = nt(kv_ref[at, HD:], grads)
            gs = (p * (gp - delta)).astype(bf16)
            acc_ref[...] += tn(kv_ref[at, :HD], gs)
            to_ref[to, :HD] = (nn(gs, queries) * scale).astype(bf16)
            to_ref[to, HD:] = nn(p.astype(bf16), grads).astype(bf16)

        @pl.when(flags[n] == 0)
        def _():
            to_ref[to, :] = jnp.zeros((block, 2 * HD), bf16)

    out = acc_ref[...].T * scale
    cosine, sine = cos_ref[...], -sin_ref[...]
    gq_ref[:, :HD] = turned(out[:block], cosine, sine).astype(bf16)
    gq_ref[:, HD:] = turned(out[block:], cosine, sine).astype(bf16)


def attend_back(flags, places, bias, queries, kv, mixed, grad_mixed, lse, cosine, sine, m, block):
    tokens, cols = kv.shape
    heads = cols // (2 * HD)
    keys = bias.shape[0]
    near = (near_count(block) + 1) * block
    own = pl.BlockSpec((block, 2 * HD), lambda h: (0, h))
    far = pl.BlockSpec((keys - near, 2 * HD), lambda h: (0, h))
    close = pl.BlockSpec((near, 2 * HD), lambda h: (0, h))
    return pl.pallas_call(
        attend_back_kernel,
        out_shape=(
            jax.ShapeDtypeStruct((block, cols), bf16),
            jax.ShapeDtypeStruct((keys - near, cols), bf16),
            jax.ShapeDtypeStruct((near, cols), bf16),
        ),
        grid=(heads,),
        in_specs=[
            pl.BlockSpec(memory_space=pltpu.SMEM),
            pl.BlockSpec(memory_space=pltpu.SMEM),
            pl.BlockSpec((keys, block), lambda h: (0, 0)),
            pl.BlockSpec((block, 2 * HD), lambda h: (m, h)),
            pl.BlockSpec((tokens, 2 * HD), lambda h: (0, h)),
            own,
            own,
            pl.BlockSpec((1, 1, 2 * block), lambda h: (h, 0, 0)),
            pl.BlockSpec((block, HD), lambda h: (m, 0)),
            pl.BlockSpec((block, HD), lambda h: (m, 0)),
        ],
        out_specs=(own, far, close),
        scratch_shapes=[pltpu.VMEM((HD, 2 * block), f32)],
        compiler_params=pltpu.CompilerParams(vmem_limit_bytes=40 * MIB),
        cost_estimate=SMALL,
    )(flags, places, bias, queries, kv, mixed, grad_mixed, lse, cosine, sine)


FCOLS = 256
FROWS = 512


def ffn_kernel(b_ref, gz_ref, wg_ref, wu_ref, wd_ref, act_ref, grads_ref, y_ref, gb_ref, yacc, gacc):
    step = pl.program_id(0)
    last = pl.num_programs(0) - 1

    @pl.when(step == 0)
    def _():
        yacc[...] = jnp.zeros_like(yacc)
        gacc[...] = jnp.zeros_like(gacc)

    def body(i, carry):
        at = pl.ds(pl.multiple_of(i * FROWS, FROWS), FROWS)
        w = jnp.concatenate([wg_ref[...], wu_ref[...]], axis=1)
        both = nn(b_ref[at, :], w)
        gate, up = both[:, :FCOLS], both[:, FCOLS:]
        grad_act = nt(gz_ref[0, at, :], wd_ref[...])
        sigma = jax.nn.sigmoid(gate)
        swish = gate * sigma
        act = (swish * up).astype(bf16)
        grad_gate = (grad_act * up * sigma * (1.0 + gate * (1.0 - sigma))).astype(bf16)
        grad_up = (grad_act * swish).astype(bf16)
        act_ref[at, :] = act
        grads_ref[0, at, :] = grad_gate
        grads_ref[1, at, :] = grad_up
        yacc[at, :] += nn(act, wd_ref[...])
        gacc[at, :] += nt(jnp.concatenate([grad_gate, grad_up], axis=1), w)
        return carry

    lax.fori_loop(0, b_ref.shape[0] // FROWS, body, 0)

    @pl.when(step == last)
    def _():
        y_ref[...] = yacc[...].astype(bf16)
        gb_ref[...] = gacc[...].astype(bf16)


def feed_forward(b, gz, gate_up, down, m, batches, kept):
    count, width = b.shape
    cols = down.shape[0]
    steps = cols // FCOLS
    once = pl.Buffered(1)
    wide = jax.ShapeDtypeStruct((batches * count, cols), bf16)
    narrow = jax.ShapeDtypeStruct((count, width), bf16)
    tile = pl.BlockSpec((count, FCOLS), lambda j: (m, j))
    total = pl.BlockSpec((count, width), lambda j: (0, 0), pipeline_mode=once)

    def kernel(*refs):
        ffn_kernel(*refs[:5], *refs[5 + len(kept) :])

    return pl.pallas_call(
        kernel,
        out_shape=(wide, jax.ShapeDtypeStruct((2,) + wide.shape, bf16), narrow, narrow),
        grid=(steps,),
        in_specs=[
            pl.BlockSpec((count, width), lambda j: (0, 0), pipeline_mode=once),
            pl.BlockSpec((1, count, width), lambda j: (0, 0, 0), pipeline_mode=once),
            pl.BlockSpec((width, FCOLS), lambda j: (0, j)),
            pl.BlockSpec((width, FCOLS), lambda j: (0, j + steps)),
            pl.BlockSpec((FCOLS, width), lambda j: (j, 0)),
        ]
        + [pl.BlockSpec(memory_space=pl.ANY)] * len(kept),
        out_specs=(tile, pl.BlockSpec((2, count, FCOLS), lambda j: (0, m, j)), total, total),
        scratch_shapes=[pltpu.VMEM((count, width), f32), pltpu.VMEM((count, width), f32)],
        input_output_aliases={5 + i: i for i in range(len(kept))},
        compiler_params=pltpu.CompilerParams(vmem_limit_bytes=60 * MIB),
        cost_estimate=SMALL,
    )(b, gz, gate_up, gate_up, down, *kept)


def plane():
    return lax.axis_size("fsdp")


def bits_of(n):
    return [1 << i for i in range(n.bit_length() - 1)]


def fswap(bits):
    return lambda value: lax.ppermute(value, "fsdp", [(i, i ^ bits) for i in range(plane())])


def cswap(bits):
    return lambda value: lax.ppermute(value, "ctx", [(i, i ^ bits) for i in range(lax.axis_size("ctx"))])


def move(pairs):
    pairs = list(pairs)
    return lambda value: lax.ppermute(value, "ctx", pairs)


def rows(value, start, size):
    return lax.dynamic_slice_in_dim(value, start, size, axis=0)


def put_rows(target, value, start):
    return lax.dynamic_update_slice_in_dim(target, value, start, axis=0)


def plus(left, right):
    return left.astype(f32) + right.astype(f32)


def joined(parts):
    return jnp.concatenate(parts, axis=0) if len(parts) > 1 else parts[0]


def blank(rows_count, cols, kind, source):
    anywhere = pl.BlockSpec(memory_space=pl.ANY)
    return pl.pallas_call(
        lambda source_ref, out_ref: None,
        out_shape=jax.ShapeDtypeStruct((rows_count, cols), kind),
        in_specs=[anywhere],
        out_specs=anywhere,
    )(source)


def gate(values):
    if len(values) < 2:
        return list(values)
    anywhere = pl.BlockSpec(memory_space=pl.ANY)
    out = pl.pallas_call(
        lambda *refs: None,
        out_shape=[jax.ShapeDtypeStruct(v.shape, v.dtype) for v in values],
        in_specs=[anywhere] * len(values),
        out_specs=[anywhere] * len(values),
        input_output_aliases={i: i for i in range(len(values))},
        cost_estimate=SMALL,
    )(*values)
    return list(out)


class Flow:
    def __init__(self, steps, fresh=False):
        self.steps, self.result, self.want, self.got = steps, None, [], None
        self.fresh = fresh
        self.go(None)

    def go(self, given):
        try:
            self.want = self.steps.send(given)
        except StopIteration as stop:
            self.want, self.result = [], stop.value


class Line:
    def __init__(self):
        self.under_way = []

    def launch(self, *flows):
        flows = [f for f in flows if f.want]
        ready = gate([value for f in flows if f.fresh for value, _ in f.want])
        for f in flows:
            f.got = [fn(ready.pop(0) if f.fresh else value) for value, fn in f.want]
            self.under_way.append(f)

    def settle(self, *held):
        gated = gate([a for f in self.under_way for a in f.got] + list(held))
        for f in self.under_way:
            given, gated = gated[: len(f.got)], gated[len(f.got) :]
            f.go(given)
        self.under_way = []
        return gated[0] if len(held) == 1 else gated

    def finish(self, *flows):
        if self.under_way:
            self.settle()
        while any(f.want for f in flows):
            self.launch(*flows)
            self.settle()


def order():
    out = []
    for bits in (bits_of(plane()), bits_of(plane())[::-1]):
        ds = [0]
        for b in bits:
            ds = ds + [d ^ b for d in ds]
        out += ds
    return out


def gather_flow(own):
    half = own.shape[0] // 2
    first, last = own[:half], own[half:]
    bits = bits_of(plane())
    for a, b in zip(bits, bits[::-1]):
        got = yield [(first, fswap(a)), (last, fswap(b))]
        first = joined([first, got[0]])
        last = joined([last, got[1]])
    return joined([first, last])


def scatter_flow(parts):
    total = parts.shape[0] // 2
    first, last = parts[:total], parts[total:]
    bits = bits_of(plane())
    for a, b in zip(bits[::-1], bits):
        n = first.shape[0] // 2
        got = yield [(first[n:].astype(bf16), fswap(a)), (last[n:].astype(bf16), fswap(b))]
        first = plus(first[:n], got[0])
        last = plus(last[:n], got[1])
    return joined([first, last])


def weight_flow(own):
    shard, cols = own.shape
    me = lax.axis_index("fsdp")
    core = lax.axis_index("ctx") % 2
    half, part = shard // 2, shard // 4
    full = None
    mine = rows(own, core * half, half)
    first, last = mine[:part], mine[part:]
    bits = bits_of(plane())
    held, pending = [0], []
    for a, b in zip(bits + [None], bits[::-1] + [None]):
        want = [(value, cswap(1)) for value, _, _ in pending]
        if a is not None:
            want += [(first, fswap(a)), (last, fswap(b))]
        got = yield want
        if full is None:
            full = put_rows(blank(shard * plane(), cols, bf16, got[0]), own, me * shard)
        for n, (here, ds, offset) in enumerate(pending):
            for k, d in enumerate(ds):
                at = slice(k * part, (k + 1) * part)
                start = (me ^ d) * shard + offset
                full = put_rows(full, here[at], start + core * half)
                full = put_rows(full, got[n][at], start + (1 - core) * half)
        if a is not None:
            order_a = held_of(bits[: bits.index(a)])
            order_b = held_of(bits[::-1][: bits[::-1].index(b)])
            n = len(pending)
            pending = [
                (got[n], [d ^ a for d in order_a], 0),
                (got[n + 1], [d ^ b for d in order_b], part),
            ]
            first = joined([first, got[n]])
            last = joined([last, got[n + 1]])
    return full


def held_of(bits):
    ds = [0]
    for b in bits:
        ds = ds + [d ^ b for d in ds]
    return ds


def column_flow(weights, full, left):
    me = lax.axis_index("fsdp")
    core = lax.axis_index("ctx") % 2
    planes = plane()
    shard = weights.shape[0]
    half = shard // 2
    size = weights.shape[1] // planes

    def columns(j, start, count):
        return lax.dynamic_slice(weights, (start, (me ^ j) * size), (count, size))

    got = yield [(columns(j, core * half, half), fswap(j)) for j in range(1, planes)]
    full[0] = lax.dynamic_update_slice(full[0], columns(0, 0, shard), (me * shard, left))
    other = yield [(piece, cswap(1)) for piece in got]
    for j in range(1, planes):
        start = (me ^ j) * shard
        full[0] = lax.dynamic_update_slice(full[0], got[j - 1], (start + core * half, left))
        full[0] = lax.dynamic_update_slice(full[0], other[j - 1], (start + (1 - core) * half, left))
    return None


def shared_bits():
    bits = bits_of(lax.axis_size("ctx"))
    return bits[1:-1] + bits[:1]


def near_count(block):
    return -(-(LONGEST - 1) // block)


def slot_blocks(block):
    n = lax.axis_size("ctx")
    half = n // 2
    ctx = lax.axis_index("ctx")
    places = [((ctx % half) ^ d, True) for d in held_of(shared_bits())]
    count = near_count(block)
    return places + [(ctx - d, ctx - d >= half) for d in list(range(1, count + 1)) + [0]]


def keys_back_flow(shared, near):
    n = lax.axis_size("ctx")
    half = n // 2
    block = shared.shape[0] // half
    count = near_count(block)
    held = shared
    for b in reversed(shared_bits()):
        m = held.shape[0] // 2
        got = yield [(held[m:], cswap(b))]
        held = plus(held[:m], got[0]).astype(bf16)
    got = yield [(held, move((c + half, c) for c in range(half)))] + [
        (near[(d - 1) * block : d * block], move((c, c - d) for c in range(half + d, n))) for d in range(1, count + 1)
    ]
    prompt = plus(held, got[0])
    own = near[count * block :].astype(f32)
    for arrived in got[1:]:
        own = own + arrived.astype(f32)
    return jnp.where(lax.axis_index("ctx") < half, prompt, own).astype(bf16)


def core_flow(value, axis):
    size = value.shape[axis] // 2
    mine = (lax.axis_index("ctx") % 2) * size
    keep = lax.dynamic_slice_in_dim(value, mine, size, axis=axis)
    send = lax.dynamic_slice_in_dim(value, size - mine, size, axis=axis)
    got = yield [(send, cswap(1))]
    return plus(keep, got[0]).astype(bf16)


def rows_flow(partial):
    planes = plane()
    me = lax.axis_index("fsdp")
    shard, cols = partial.shape[0] // planes, partial.shape[1]
    p = yield from core_flow(partial.reshape(planes, shard, cols), 1)
    p = p.reshape(2 * planes, shard // 4, cols)
    p = joined([rows(p, (me ^ j) * 2 + n // planes, 1)[0] for n, j in enumerate(order())])
    s = yield from scatter_flow(p)
    return s.astype(bf16)


def cores_flow(half, widths):
    core = lax.axis_index("ctx") % 2
    count = half.shape[0]
    (other,) = yield [(half, cswap(1))]
    outs, left = [], 0
    for width in widths:
        out = blank(2 * count, width, f32, outs[-1] if outs else other)
        for source, start in ((half, core * count), (other, (1 - core) * count)):
            out = put_rows(out, source[:, left : left + width].astype(f32), start)
        outs.append(out)
        left += width
    return outs


def direct_flow(value, widths):
    chips = lax.axis_size("ctx") // 2
    place = lax.axis_index("ctx") // 2
    size = value.shape[0] // chips
    others = range(1, chips)
    got = yield [(rows(value, (place ^ d) * size, size), cswap(2 * d)) for d in others]
    own = rows(value, place * size, size).astype(f32)
    for arrived in got:
        own = own + arrived.astype(f32)
    own = own.astype(bf16)
    got = yield [(own, cswap(2 * d)) for d in others]
    half = put_rows(blank(value.shape[0], value.shape[1], bf16, got[0]), own, place * size)
    for d, arrived in zip(others, got):
        half = put_rows(half, arrived, (place ^ d) * size)
    return (yield from cores_flow(half, widths))


def exchange_flow(own, stack):
    planes, size, cols = own.shape
    me = lax.axis_index("fsdp")
    pieces = [lax.dynamic_index_in_dim(own, me ^ j, 0, keepdims=False) for j in range(planes)]
    got = yield [(pieces[j], fswap(j)) for j in range(1, planes)]
    line = blank(size, planes * cols, bf16, got[0])
    width = cols // stack
    for j, piece in enumerate(pieces[:1] + got):
        for n in range(stack):
            part = piece[:, n * width : (n + 1) * width]
            line = lax.dynamic_update_slice(line, part, (0, n * planes * width + (me ^ j) * width))
    return line


def total_flow(value):
    for fn in [cswap(b) for b in bits_of(lax.axis_size("ctx"))] + [fswap(b) for b in bits_of(plane())]:
        got = yield [(value, fn)]
        value = value + got[0]
    return value


def local(
    hidden_in,
    cotangent,
    segment_ids,
    w_query,
    w_key,
    w_value,
    w_output,
    w_gate,
    w_up,
    w_down,
    attn_gain,
    ffn_gain,
):
    batches, block, width = hidden_in.shape
    tokens = segment_ids.shape[1]
    ctx = lax.axis_index("ctx")
    planes = plane()
    me = lax.axis_index("fsdp")
    first_row = ctx * block
    qd = w_query.shape[1]
    kvd = w_key.shape[1]
    shard = w_query.shape[0]
    ff_own = w_down.shape[0]
    groups = range(batches)

    line = Line()
    keys_weight = Flow(weight_flow(jnp.concatenate([w_key, w_value], axis=1)))
    query_weight = Flow(weight_flow(w_query))
    out_weight = Flow(weight_flow(w_output))
    gate_up = [blank(width, 2 * ff_own, bf16, w_gate)]
    gate_weight = Flow(column_flow(w_gate, gate_up, 0))
    up_weight = Flow(column_flow(w_up, gate_up, ff_own))
    gz = [Flow(gather_flow(cotangent[m])) for m in groups]

    line.launch(keys_weight)
    gains_own = jnp.stack([attn_gain, ffn_gain])
    gains = jnp.zeros((2, width), bf16)
    for j in range(planes):
        piece = fswap(j)(gains_own) if j else gains_own
        gains = lax.dynamic_update_slice(gains, piece, (0, (me ^ j) * shard))
    gains = gains.astype(f32)
    gain_attn, gain_ffn = gains[0], gains[1]
    segment_ids = line.settle(segment_ids)
    segments_later = segment_ids

    line.launch(keys_weight)
    hidden = hidden_in.reshape(batches * block, width).astype(f32)
    normed_attn, scaled_attn, inverse_attn = norm_parts(hidden, gain_attn)
    attn_in = normed_attn.astype(bf16)
    tables = [rotary_tables(positions_of(segment_ids[m], first_row, block)) for m in groups]
    cosine = joined([t[0] for t in tables])
    sine = joined([t[1] for t in tables])
    line.settle()

    line.launch(keys_weight, query_weight)
    line.settle()
    line.finish(keys_weight)
    line.launch(query_weight, out_weight)
    kv_own = project(attn_in, keys_weight.result, cosine, sine, False)
    kv_own, segments_later = line.settle(kv_own, segments_later + 0)
    keys = [lax.all_gather(kv_own[m * block : (m + 1) * block], "ctx", axis=0, tiled=True) for m in groups]
    line.launch(query_weight, out_weight, *gz)
    line.settle()
    line.finish(query_weight)
    line.launch(out_weight, gate_weight)
    queries = project(attn_in, query_weight.result, cosine, sine, True)

    slots = slot_blocks(block)
    places = jnp.stack([jnp.where(counts, p, 0) for p, counts in slots])
    after_all = jnp.stack([jnp.where(counts, 0, tokens) for _, counts in slots])
    within = jnp.arange(block, dtype=i32)
    query_index = first_row + within
    key_index = (places[:, None] * block + after_all[:, None] + within[None, :]).reshape(-1)
    biases, flags = [], []
    for m in groups:
        segments = segments_later[m]
        query_segments = lax.dynamic_slice_in_dim(segments, first_row, block)
        chosen = (places[:, None] == jnp.arange(tokens // block, dtype=i32)[None, :]).astype(i32)
        key_segments = jnp.sum(chosen[:, :, None] * segments.reshape(1, -1, block), axis=1).reshape(-1)
        visible = (key_index[:, None] <= query_index[None, :]) & (
            (key_segments[:, None] == query_segments[None, :]) | (key_segments[:, None] == 0)
        )
        biases.append(jnp.where(visible, 0.0, mask_fill).astype(f32))
        flags.append(jnp.any(visible.reshape(-1, block * block), axis=1).astype(i32))

    mixed, lses, middles, normed, b_flows = [], [], [], [], []

    def attention(m):
        o, lse = line.settle(*attend(flags[m], places, biases[m], queries, keys[m], m, block))
        mixed.append(o)
        lses.append(lse)

    def to_feed_forward(m):
        middle = hidden[m * block : (m + 1) * block] + nn(mixed[m], out_weight.result)
        normed_ffn, scaled, inverse = norm_parts(middle, gain_ffn)
        middles.append(middle)
        normed.append((scaled, inverse))
        b_flows.append(Flow(gather_flow(normed_ffn.astype(bf16))))

    attention(0)
    line.finish(out_weight)
    line.launch(gate_weight, up_weight, *gz)
    to_feed_forward(0)
    for m in groups[1:]:
        attention(m)
        line.launch(*b_flows, up_weight)
        to_feed_forward(m)
    line.settle()
    line.launch(*b_flows)
    line.settle()

    wide, out_parts, grad_flows, b_all = (), [], [], []
    line.finish(gate_weight, up_weight)
    for m in groups:
        line.finish(b_flows[m], gz[m])
        line.launch(*b_flows, *grad_flows)
        b = b_flows[m].result
        b_all.append(b)
        *wide, out_part, grad_part = feed_forward(b, gz[m].result[None], gate_up[0], w_down, m, batches, tuple(wide))
        out_part, grad_part = line.settle(out_part, grad_part)
        out_parts.append(Flow(scatter_flow(out_part), True))
        grad_flows.append(Flow(scatter_flow(grad_part), True))
    act, grad_wide = wide

    line.launch(*grad_flows)
    grad_up = line.settle(product(joined(b_all), grad_wide))
    up_part = lax.psum_scatter(
        grad_up.reshape(planes, shard, 2 * ff_own), "ctx", scatter_dimension=1, tiled=True
    )
    line.launch(*grad_flows)
    line.settle()
    line.finish(*grad_flows)

    grad_middles, gys, grads_mixed = [], [], []
    grad_ffn_gain = jnp.zeros((width,), f32)
    for m in groups:
        scaled, inverse = normed[m]
        grad_part, gain_part = norm_back(grad_flows[m].result, middles[m], scaled, inverse, gain_ffn)
        grad_ffn_gain = grad_ffn_gain + gain_part
        grad_middle = cotangent[m].astype(f32) + grad_part
        gy = grad_middle.astype(bf16)
        grads_mixed.append(nt(gy, out_weight.result).astype(bf16))
        grad_middles.append(grad_middle)
        gys.append(gy)
    key_backs, grads_q = [], []
    for m in groups:
        line.launch(*key_backs)
        gq, *gkv = attend_back(
            flags[m], places, biases[m], queries, keys[m], mixed[m], grads_mixed[m], lses[m], cosine, sine, m, block
        )
        if m + 1 < batches:
            gq, *gkv, grads_mixed[-1] = line.settle(gq, *gkv, grads_mixed[-1])
        else:
            gq, *gkv = line.settle(gq, *gkv)
        grads_q.append(gq)
        key_backs.append(Flow(keys_back_flow(*gkv), True))

    gq = joined(grads_q)
    line.launch(*key_backs, *out_parts)
    grad_down = product(act, joined([f.result for f in gz]))
    grad_attn = product(jnp.stack([attn_in, joined(mixed)]), jnp.stack([gq, joined(gys)]))
    grad_down, grad_attn, up_part = line.settle(grad_down, grad_attn, up_part)
    down_part = lax.psum_scatter(grad_down, "ctx", scatter_dimension=0, tiled=True)
    grad_attn = Flow(rows_flow(grad_attn), True)
    up_line = Flow(exchange_flow(up_part, 2))
    line.launch(*key_backs, grad_attn, up_line)
    line.settle()
    line.finish(up_line)
    line.launch(*key_backs, grad_attn, *out_parts)
    up_row = line.settle(up_line.result)
    up_all = lax.all_gather(up_row, "ctx", axis=0, tiled=True)
    line.finish(*key_backs)
    line.launch(grad_attn)
    gkv = unturn(joined([f.result for f in key_backs]), cosine, sine)
    grad_keys, gkv, down_part = line.settle(product(attn_in, gkv), gkv, down_part)
    grad_keys = Flow(rows_flow(grad_keys), True)
    line.finish(grad_attn)
    line.launch(grad_keys)
    grad_attn_in = nt(gq, query_weight.result) + nt(gkv, keys_weight.result)
    grad_part, grad_attn_gain = norm_back(grad_attn_in, hidden, scaled_attn, inverse_attn, gain_attn)
    grad_in = (joined(grad_middles) + grad_part).astype(bf16)
    gain_grads, down_part = line.settle(jnp.stack([grad_attn_gain, grad_ffn_gain]), down_part)
    gains_back = Flow(total_flow(gain_grads))
    line.launch(grad_keys, gains_back)
    down_part = line.settle(down_part)
    down_all = lax.all_gather(down_part, "ctx", axis=0, tiled=True)
    line.launch(grad_keys, gains_back)
    line.settle()
    line.finish(grad_keys)
    both = jnp.concatenate([grad_attn.result, grad_keys.result], axis=1)
    attn_out = Flow(direct_flow(both, [qd, width, kvd, kvd]))
    line.launch(attn_out, gains_back)
    up_all = line.settle(up_all)
    grad_gate = up_all[:, : planes * ff_own].astype(f32)
    grad_up = up_all[:, planes * ff_own :].astype(f32)
    line.launch(attn_out, gains_back, *out_parts)
    grad_gate, grad_up, down_all = line.settle(grad_gate, grad_up, down_all)
    grad_down = down_all.astype(f32)
    line.launch(attn_out, gains_back, *out_parts)
    grad_down = line.settle(grad_down)
    line.finish(attn_out, gains_back, *out_parts)
    gain_grads = lax.dynamic_slice(gains_back.result, (0, me * shard), (2, shard))
    outputs = [(middles[m] + out_parts[m].result).astype(bf16) for m in groups]
    return (
        jnp.stack(outputs),
        grad_in.reshape(batches, block, width),
        attn_out.result[0],
        attn_out.result[2],
        attn_out.result[3],
        attn_out.result[1],
        grad_gate,
        grad_up,
        grad_down,
        gain_grads[0],
        gain_grads[1],
    )


def solution(mesh):
    tokens3 = P("fsdp", "ctx", None)
    matrix = P("fsdp", None)
    return jax.shard_map(
        local,
        mesh=mesh,
        in_specs=(tokens3, tokens3) + (matrix,) * 8 + (P("fsdp"),) * 2,
        out_specs=(tokens3, tokens3) + (matrix,) * 7 + (P("fsdp"),) * 2,
        check_vma=False,
    )
```
